512 devices in a mesh: row: 16 (over x_hi, y), col: 8 (over z), layer: 4 (over x_lo, core).
Axes of the slice: x: 4 (x_hi: 2, x_lo: 2; x = x_hi * 2 + x_lo), y: 8, z: 8, core: 2. Of those that a mesh axis runs over, the one named last changes fastest.
Arguments:
- a_blocks: bfloat16 [16, 8, 4, 24, 128, 128], P('row', 'col', 'layer'), may hold values from -0.5 to 0.5
- a_index: int32 [16, 8, 4, 2, 24], P('row', 'col', 'layer'), may hold values from 0 to 511, as said below
- a_send: int32 [16, 8, 4, 8, 3], P('row', 'col', 'layer'), may hold values from 0 to 23, as said below
- a_count: int32 [16, 8, 4, 8], P('row', 'col', 'layer'), may hold values from 1 to 3, as said below
- b_blocks: bfloat16 [16, 8, 4, 16, 128, 128], P('row', 'col', 'layer'), may hold values from -6 to 6
- b_index: int32 [16, 8, 4, 2, 16], P('row', 'col', 'layer'), may hold values from 0 to 511, as said below
- b_send: int32 [16, 8, 4, 16, 2], P('row', 'col', 'layer'), may hold values from 0 to 15, as said below
- b_count: int32 [16, 8, 4, 16], P('row', 'col', 'layer'), may hold values from 0 to 2, as said below
- c_index: int32 [16, 8, 2, 24], P('row', 'col'), may hold values from 0 to 511, as said below
Outputs:
- product: bfloat16 [16, 8, 24, 128, 128], P('row', 'col', 'layer')
The draws below stay inside these ranges and needn't reach their ends.
Inputs may be any that keep to these rules, and one draw needn't show every extreme that they name: `a_index`: every slot of a device is named by exactly one entry of its send lists. A slot named in list d of device (r, c, l) holds a block (i, k) with i % 16 = r, k % (32) = 8 * l + (r + d) % 8. `a_send`: each device's lists together name each of its 24 slots exactly once. `a_count`: in every draw some device receives 3 live blocks from every device of its row and layer. `b_index`: A slot named in list q of device (r, c, l) holds a block (k, j) with j % 8 = c and k % (32) = 8 * l + (q + c) % 8. No two live blocks of B share a position, and no block row of B holds more than 2 live blocks whose block columns are equal modulo 8; in every draw some such group holds 2. `b_send`: the lists of device (r, c, l) for rows q and q + 8 are equal, lists for rows that differ modulo 8 name disjoint slots, and together they name each of the 16 slots once. `b_count`: the counts for rows q and q + 8 are equal. In every draw some device receives 2 live blocks from every device of its column and layer. `c_index`: the kept blocks of cell (r, c) are distinct and have block row i with i % 16 = r and block column j with j % 8 = c.
All inputs are finite; a program needn't handle non-finite values.
Results may differ from the reference program's by a relative error of at most 0.012.
Values may be sent and summed in bfloat16 or wider, within the bound.
A program may use at most 128 MiB of HBM per device.

```python
import math
import jax
import jax.numpy as jnp
from jax import lax

BLOCK = 128
MATRIX_BLOCKS = 512
A_HELD = 24
B_MOST = 2
C_KEPT = 24
GRID_ROWS = 16
GRID_COLS = 8
LAYERS = 4
K_ROWS = 16
ROW_BLOCKS = 32
COL_BLOCKS = 64
CAP_A = 3
CAP_B = 2
B_STORE = 16
N_ROW = 16
N_COL = 8
N_LAYER = 4


def distinct_order(key, shape, length):
    spread = jax.random.randint(key, shape + (length,), 0, 1 << 14)
    scores = spread * length + lax.broadcasted_iota(jnp.int32, shape + (length,), len(shape))
    return jnp.argsort(scores, axis=-1).astype(jnp.int32)


def grid_iota(shape, axis):
    return lax.broadcasted_iota(jnp.int32, shape, axis)


def structure(key):
    subkeys = jax.random.split(key, 11)
    part_count = GRID_COLS * LAYERS
    row_step = ROW_BLOCKS // K_ROWS
    col_step = COL_BLOCKS // K_ROWS
    entry_shape = (GRID_ROWS, GRID_COLS, LAYERS, GRID_COLS, CAP_A)
    count_shape = (GRID_ROWS, GRID_COLS, LAYERS, GRID_COLS)
    counts_a = jax.random.randint(subkeys[0], count_shape, 1, CAP_A + 1)
    chosen_a = jax.random.randint(subkeys[1], (3,), 0, jnp.array([GRID_ROWS, LAYERS, GRID_COLS], jnp.int32))
    full_a = (grid_iota(count_shape, 0) == chosen_a[0]) & (grid_iota(count_shape, 2) == chosen_a[1]) & (grid_iota(count_shape, 3) == chosen_a[2])
    counts_a = jnp.where(full_a, CAP_A, counts_a).astype(jnp.int32)
    order_a = distinct_order(subkeys[2], (GRID_ROWS, GRID_COLS, LAYERS), A_HELD)
    send_a = order_a.reshape(entry_shape)
    band_a = jax.random.randint(subkeys[3], entry_shape, 0, K_ROWS)
    near_a = jax.random.randint(subkeys[4], entry_shape, 0, row_step)
    row_pos = grid_iota(entry_shape, 0)
    layer_pos = grid_iota(entry_shape, 2)
    dest_pos = grid_iota(entry_shape, 3)
    local_a = row_step * band_a + near_a
    row_a = GRID_ROWS * local_a + row_pos
    column_a = part_count * band_a + GRID_COLS * layer_pos + (row_pos + dest_pos) % GRID_COLS
    live_a = (grid_iota(entry_shape, 4) < counts_a[..., None]).astype(jnp.int32)
    inverse_a = jnp.argsort(order_a, axis=-1)
    flat_shape = (GRID_ROWS, GRID_COLS, LAYERS, A_HELD)
    index_a = jnp.stack([jnp.take_along_axis(row_a.reshape(flat_shape), inverse_a, axis=-1), jnp.take_along_axis(column_a.reshape(flat_shape), inverse_a, axis=-1)], axis=3).astype(jnp.int32)
    class_shape = (GRID_COLS, GRID_COLS, LAYERS)
    counts_b = jax.random.randint(subkeys[5], class_shape + (K_ROWS,), 1, B_MOST + 1)
    chosen_b = jax.random.randint(subkeys[6], (3,), 0, jnp.array([GRID_COLS, GRID_COLS, LAYERS], jnp.int32))
    full_b = (grid_iota(class_shape, 0) == chosen_b[0]) & (grid_iota(class_shape, 1) == chosen_b[1]) & (grid_iota(class_shape, 2) == chosen_b[2])
    counts_b = jnp.where(full_b[..., None], B_MOST, counts_b)
    spot_shape = class_shape + (K_ROWS, B_MOST)
    live_spot = (grid_iota(spot_shape, 4) < counts_b[..., None]).astype(jnp.int32)
    offset_b = distinct_order(subkeys[7], class_shape + (K_ROWS,), col_step)[..., :B_MOST]
    band_b = grid_iota(spot_shape, 3)
    class_pos = grid_iota(spot_shape, 0)
    column_pos = grid_iota(spot_shape, 1)
    layer_b = grid_iota(spot_shape, 2)
    local_b = col_step * band_b + offset_b
    row_b = part_count * band_b + GRID_COLS * layer_b + (class_pos + column_pos) % GRID_COLS
    column_b = GRID_COLS * local_b + column_pos
    spots = K_ROWS * B_MOST
    placing = distinct_order(subkeys[8], class_shape, spots)
    from_slot = jnp.argsort(placing, axis=-1)
    slot_shape = class_shape + (GRID_ROWS, CAP_B)

    def by_slot(values):
        return jnp.take_along_axis(values.reshape(class_shape + (spots,)), from_slot, axis=-1).reshape(slot_shape)
    live_slot = by_slot(live_spot)
    row_slot = by_slot(row_b)
    column_slot = by_slot(column_b)
    listing = jnp.argsort((1 - live_slot) * CAP_B + grid_iota(slot_shape, 4), axis=-1)

    def listed(values):
        return jnp.transpose(jnp.take_along_axis(values, listing, axis=-1), (3, 1, 2, 0, 4))
    count_class = jnp.transpose(jnp.sum(live_slot, axis=-1), (3, 1, 2, 0))
    storing = distinct_order(subkeys[9], (GRID_ROWS, GRID_COLS, LAYERS), B_STORE)
    store_split = storing.reshape(GRID_ROWS, GRID_COLS, LAYERS, GRID_COLS, CAP_B)
    copies = jnp.arange(GRID_ROWS) % GRID_COLS
    send_b = store_split[:, :, :, copies, :].astype(jnp.int32)
    count_b = count_class[:, :, :, copies].astype(jnp.int32)
    inverse_b = jnp.argsort(storing, axis=-1)
    store_shape = (GRID_ROWS, GRID_COLS, LAYERS, B_STORE)
    index_b = jnp.stack([jnp.take_along_axis(listed(row_slot).reshape(store_shape), inverse_b, axis=-1), jnp.take_along_axis(listed(column_slot).reshape(store_shape), inverse_b, axis=-1)], axis=3).astype(jnp.int32)
    pattern_a = jnp.zeros((GRID_ROWS, ROW_BLOCKS, MATRIX_BLOCKS), jnp.int32).at[row_pos, local_a, column_a].add(live_a)
    pattern_b = jnp.zeros((GRID_COLS, MATRIX_BLOCKS, COL_BLOCKS), jnp.int32).at[column_pos, row_b, local_b].add(live_spot)
    meeting = jnp.einsum('ruk,ckv->rcuv', pattern_a, pattern_b)
    region = ROW_BLOCKS * COL_BLOCKS
    tiebreak = distinct_order(subkeys[10], (GRID_ROWS, GRID_COLS), region)
    score = meeting.reshape(GRID_ROWS, GRID_COLS, region) * region + tiebreak
    chosen = lax.top_k(score, C_KEPT)[1].astype(jnp.int32)
    cell_shape = (GRID_ROWS, GRID_COLS, C_KEPT)
    index_c = jnp.stack([GRID_ROWS * (chosen // COL_BLOCKS) + grid_iota(cell_shape, 0), GRID_COLS * (chosen % COL_BLOCKS) + grid_iota(cell_shape, 1)], axis=2).astype(jnp.int32)
    return (index_a, send_a, counts_a, index_b, send_b, count_b, index_c)


def draw_a_index(key, part):
    return structure(key)[0]


def draw_a_send(key, part):
    return structure(key)[1]


def draw_a_count(key, part):
    return structure(key)[2]


def draw_b_index(key, part):
    return structure(key)[3]


def draw_b_send(key, part):
    return structure(key)[4]


def draw_b_count(key, part):
    return structure(key)[5]


def draw_c_index(key, part):
    return structure(key)[6]


def levels(key, shape, cuts, least, top_value):
    factor_of = 1.0
    for axis_at, blocks in cuts:
        steps = jax.random.uniform(jax.random.fold_in(jax.random.fold_in(key, 6), axis_at), (blocks,), jnp.float32, least / len(cuts), top_value / len(cuts))
        factor_of = factor_of * jnp.repeat(jnp.exp(steps), shape[axis_at] // blocks).reshape((-1,) + (1,) * (len(shape) - 1 - axis_at))
    return factor_of


def gaussian(rng, extent, scale, limit, shards=(), held_as=jnp.bfloat16):
    drawn = scale * jax.random.normal(rng, extent, jnp.float32)
    if shards:
        drawn = drawn * levels(rng, extent, shards, -0.22, 0.18)
    return jnp.clip(drawn, -limit, limit).astype(held_as)


def setup_inputs(seed: int = 0) -> dict:
    key_list = jax.random.split(jax.random.key(seed), 10)
    return {
        "a_blocks": gaussian(key_list[0], (GRID_ROWS, GRID_COLS, LAYERS, A_HELD, BLOCK, BLOCK), BLOCK ** -0.5, 0.5, ((0, 16), (1, 8), (2, 4))),
        "a_index": draw_a_index(jax.random.fold_in(key_list[9], 71), 0),
        "a_send": draw_a_send(jax.random.fold_in(key_list[9], 71), 0),
        "a_count": draw_a_count(jax.random.fold_in(key_list[9], 71), 0),
        "b_blocks": gaussian(key_list[4], (GRID_ROWS, GRID_COLS, LAYERS, B_STORE, BLOCK, BLOCK), 1.0, 6.0, ((0, 16), (1, 8), (2, 4))),
        "b_index": draw_b_index(jax.random.fold_in(key_list[9], 71), 0),
        "b_send": draw_b_send(jax.random.fold_in(key_list[9], 71), 0),
        "b_count": draw_b_count(jax.random.fold_in(key_list[9], 71), 0),
        "c_index": draw_c_index(jax.random.fold_in(key_list[9], 71), 0),
    }


def live_slots(send_list, live_count, slot_count):
    listed = lax.broadcasted_iota(jnp.int32, send_list.shape, send_list.ndim - 1) < live_count[..., None]
    matched = (send_list[..., None] == jnp.arange(slot_count, dtype=jnp.int32)) & listed[..., None]
    return jnp.any(matched, axis=(-3, -2))


def reference(a_blocks, a_index, a_send, a_count, b_blocks, b_index, b_send, b_count, c_index):
    a_live = live_slots(a_send, a_count, A_HELD)
    b_live = live_slots(b_send, b_count, B_STORE)
    b_flat = b_blocks.reshape(-1, BLOCK, BLOCK)
    b_rows = b_index[:, :, :, 0, :].reshape(-1).astype(jnp.int32)
    b_cols = b_index[:, :, :, 1, :].reshape(-1).astype(jnp.int32)
    b_total = b_rows.shape[0]
    groups = MATRIX_BLOCKS * N_COL
    group_key = jnp.where(b_live.reshape(-1), b_rows * N_COL + b_cols % N_COL, groups).astype(jnp.int32)
    sorted_order = jnp.argsort(group_key * b_total + jnp.arange(b_total, dtype=jnp.int32)).astype(jnp.int32)
    sorted_key = group_key[sorted_order]
    group_start = jnp.searchsorted(sorted_key, sorted_key, side="left").astype(jnp.int32)
    group_rank = jnp.arange(b_total, dtype=jnp.int32) - group_start
    target = jnp.where((sorted_key < groups) & (group_rank < B_MOST), sorted_key * B_MOST + group_rank, groups * B_MOST).astype(jnp.int32)
    lookup = jnp.full((groups * B_MOST + 1,), -1, jnp.int32).at[target].set(sorted_order)
    kept_count = N_ROW * N_COL * C_KEPT
    c_rows = c_index[:, :, 0, :].reshape(-1).astype(jnp.int32)
    c_cols = c_index[:, :, 1, :].reshape(-1).astype(jnp.int32)
    slot_table = jnp.full((MATRIX_BLOCKS * MATRIX_BLOCKS,), kept_count, jnp.int32).at[c_rows * MATRIX_BLOCKS + c_cols].set(jnp.arange(kept_count, dtype=jnp.int32))
    summed = jnp.zeros((kept_count, BLOCK, BLOCK), jnp.float32)
    for layer_index in range(N_LAYER):
        layer_blocks = a_blocks[:, :, layer_index].reshape(-1, BLOCK, BLOCK)
        block_count = layer_blocks.shape[0]
        batch_size = math.gcd(block_count, 64)

        def batched(values):
            return values.reshape((block_count // batch_size, batch_size) + values.shape[1:])

        pieces = (batched(layer_blocks), batched(a_index[:, :, layer_index, 0, :].reshape(-1).astype(jnp.int32)), batched(a_index[:, :, layer_index, 1, :].reshape(-1).astype(jnp.int32)), batched(a_live[:, :, layer_index].reshape(-1)))

        def accumulate(partial_value, piece):
            a_part, a_rows, a_cols, a_alive = piece
            groups_of = a_cols[:, None] * N_COL + jnp.arange(N_COL, dtype=jnp.int32)[None, :]
            candidate = lookup[groups_of[:, :, None] * B_MOST + jnp.arange(B_MOST, dtype=jnp.int32)[None, None, :]].reshape(batch_size, -1)
            valid = (candidate >= 0) & a_alive[:, None]
            clipped = jnp.maximum(candidate, 0).astype(jnp.int32)
            operand = b_flat[clipped].astype(jnp.float32)
            destination = slot_table[a_rows[:, None] * MATRIX_BLOCKS + b_cols[clipped]]
            destination = jnp.where(valid, destination, kept_count).astype(jnp.int32)
            products = jnp.einsum("amn,abnp->abmp", a_part.astype(jnp.float32), operand)
            partial_value = partial_value.at[destination.reshape(-1)].add(products.reshape(-1, BLOCK, BLOCK), mode="drop")
            return partial_value, None

        partial_value, unused = lax.scan(accumulate, jnp.zeros((kept_count, BLOCK, BLOCK), jnp.float32), pieces)
        rounded = lax.optimization_barrier(partial_value.astype(jnp.bfloat16))
        summed = summed + rounded.astype(jnp.float32)
    return summed.astype(jnp.bfloat16).reshape(N_ROW, N_COL, C_KEPT, BLOCK, BLOCK)
```

```python
import functools

import jax
import jax.numpy as jnp
from jax import lax
from jax.experimental import pallas as pl
from jax.experimental.pallas import tpu as pltpu
from jax.sharding import PartitionSpec as P

BLOCK = 128
BATCH = 8
DEPTH = 8


def live_slots(send_list, live_count, slot_count):
    listed = lax.broadcasted_iota(jnp.int32, send_list.shape, 1) < live_count[:, None]
    slots = jnp.arange(slot_count, dtype=jnp.int32)
    return jnp.any((send_list[..., None] == slots) & listed[..., None], axis=(0, 1))


def product_list(a_code, b_code, c_index):
    c_rows, c_cols = c_index[0] // 16, c_index[1] // 8
    kept = c_rows.shape[0]
    a_inner, a_row = a_code // 32, a_code % 32
    b_inner, b_col = b_code // 64, b_code % 64
    slots = jnp.arange(kept, dtype=jnp.int32)
    slot = jnp.sum(
        jnp.where(
            (a_row[:, None, None] == c_rows) & (b_col[None, :, None] == c_cols), slots + 1, 0
        ),
        axis=2,
    )
    meets = (a_inner[:, None] == b_inner[None, :]) & (a_code >= 0)[:, None] & (slot > 0)
    position = jnp.arange(b_code.shape[0], dtype=jnp.int32)
    key = position[None, :] * 32 + slot - 1
    first = jnp.min(jnp.where(meets, key, 1 << 20), axis=1)
    last = jnp.max(jnp.where(meets, key, -1), axis=1)
    one = last >= 0
    two = one & (first != last)
    keys = jnp.concatenate([last, first])
    there = jnp.concatenate([one, two])
    a_slot = jnp.tile(jnp.arange(a_code.shape[0], dtype=jnp.int32), 2)
    total = keys.shape[0]
    entry = jnp.where(there, a_slot * 8192 + keys, 0)
    spots = jnp.arange(total, dtype=jnp.int32)
    rank = jnp.sum((there[None, :] & (spots[None, :] < spots[:, None])).astype(jnp.int32), axis=1)
    picked = there[:, None] & (rank[:, None] == spots[None, :])
    listed = jnp.sum(jnp.where(picked, entry[:, None], 0), axis=0)
    count = jnp.sum(there.astype(jnp.int32))
    return jnp.where(spots < count, listed, kept), count[None]


def product_kernel(
    list_ref, count_ref, a_ref, b_ref, out_ref, a_buffer, b_buffer, total, a_sem, b_sem
):
    kept = out_ref.shape[0]
    batches = (count_ref[0] + BATCH - 1) // BATCH

    def fetch(batch):
        spot = batch % DEPTH
        for n in range(BATCH):
            entry = list_ref[batch * BATCH + n]
            pltpu.make_async_copy(
                a_ref.at[entry // 8192], a_buffer.at[spot, n], a_sem.at[spot]
            ).start()
            pltpu.make_async_copy(
                b_ref.at[(entry // 32) % 256], b_buffer.at[spot, n], b_sem.at[spot]
            ).start()

    def prefetch(batch, carry):
        fetch(batch)
        return carry

    lax.fori_loop(0, jnp.minimum(batches, DEPTH), prefetch, 0)
    total[...] = jnp.zeros_like(total)

    def work(batch, carry):
        spot = batch % DEPTH
        pltpu.make_async_copy(a_buffer.at[spot], a_buffer.at[spot], a_sem.at[spot]).wait()
        pltpu.make_async_copy(b_buffer.at[spot], b_buffer.at[spot], b_sem.at[spot]).wait()
        products = [
            jnp.dot(
                a_buffer[spot, n], b_buffer[spot, n], preferred_element_type=jnp.float32
            )
            for n in range(BATCH)
        ]
        for n in range(BATCH):
            slot = list_ref[batch * BATCH + n] % 32
            total[slot] += products[n]

        @pl.when(batch + DEPTH < batches)
        def _():
            fetch(batch + DEPTH)

        return carry

    lax.fori_loop(0, batches, work, 0)
    out_ref[...] = total[0:kept].astype(out_ref.dtype)


def partial_product(listed, count, a_all, b_all, kept):
    smem = pl.BlockSpec(memory_space=pltpu.SMEM)
    anywhere = pl.BlockSpec(memory_space=pl.ANY)
    return pl.pallas_call(
        product_kernel,
        out_shape=jax.ShapeDtypeStruct((kept, BLOCK, BLOCK), jnp.bfloat16),
        in_specs=[smem, smem, anywhere, anywhere],
        out_specs=pl.BlockSpec(memory_space=pltpu.VMEM),
        scratch_shapes=[
            pltpu.VMEM((DEPTH, BATCH, BLOCK, BLOCK), jnp.bfloat16),
            pltpu.VMEM((DEPTH, BATCH, BLOCK, BLOCK), jnp.bfloat16),
            pltpu.VMEM((kept + 1, BLOCK, BLOCK), jnp.float32),
            pltpu.SemaphoreType.DMA((DEPTH,)),
            pltpu.SemaphoreType.DMA((DEPTH,)),
        ],
        compiler_params=pltpu.CompilerParams(vmem_limit_bytes=32 << 20),
        name="partial_product",
    )(listed, count, a_all, b_all)


def shards(a_blocks, a_index, a_send, a_count, b_blocks, b_index, b_send, b_count, c_index):
    a_own, b_own = a_blocks[0, 0, 0], b_blocks[0, 0, 0]
    a_rows, a_cols = a_index[0, 0, 0, 0], a_index[0, 0, 0, 1]
    b_rows, b_cols = b_index[0, 0, 0, 0], b_index[0, 0, 0, 1]
    a_live = live_slots(a_send[0, 0, 0], a_count[0, 0, 0], a_own.shape[0])
    b_live = live_slots(b_send[0, 0, 0], b_count[0, 0, 0], b_own.shape[0])
    a_code = jnp.where(a_live, (a_cols // 32 * 8 + a_cols % 8) * 32 + a_rows // 16, -1)
    b_code = jnp.where(b_live, (b_rows // 32 * 8 + b_rows % 8) * 64 + b_cols // 8, -1)
    a_code = lax.all_gather(a_code, "col", tiled=True)
    b_code = lax.all_gather(b_code, "row", tiled=True)
    a_all = lax.all_gather(a_own, "col", tiled=True)
    b_all = lax.all_gather(b_own, "row", tiled=True)
    listed, count = product_list(a_code, b_code, c_index[0, 0])
    partial = partial_product(listed, count, a_all, b_all, c_index.shape[3])
    result = lax.psum_scatter(partial, "layer", scatter_dimension=0, tiled=True)
    return result[None, None]


def solution(mesh):
    in_specs = (
        P("row", "col", "layer", None, None, None),
        P("row", "col", "layer", None, None),
        P("row", "col", "layer", None, None),
        P("row", "col", "layer", None),
        P("row", "col", "layer", None, None, None),
        P("row", "col", "layer", None, None),
        P("row", "col", "layer", None, None),
        P("row", "col", "layer", None),
        P("row", "col", None, None),
    )
    out_specs = P("row", "col", "layer", None, None)
    return jax.shard_map(shards, mesh=mesh, in_specs=in_specs, out_specs=out_specs, check_vma=False)
```

```python
import functools

import jax
import jax.numpy as jnp
from jax import lax
from jax.experimental import pallas as pl
from jax.experimental.pallas import tpu as pltpu
from jax.sharding import PartitionSpec as P

BLOCK = 128
BATCH = 8
DEPTH = 8
SEMAPHORES = 128
MESH = pl.DeviceIdType.MESH


def live_slots(send_list, live_count, slot_count):
    listed = lax.broadcasted_iota(jnp.int32, send_list.shape, 1) < live_count[:, None]
    slots = jnp.arange(slot_count, dtype=jnp.int32)
    return jnp.any((send_list[..., None] == slots) & listed[..., None], axis=(0, 1))


def product_list(a_code, b_code, c_index):
    c_rows, c_cols = c_index[0] // 16, c_index[1] // 8
    kept = c_rows.shape[0]
    a_inner, a_row = a_code // 32, a_code % 32
    b_inner, b_col = b_code // 64, b_code % 64
    slots = jnp.arange(kept, dtype=jnp.int32)
    slot = jnp.sum(
        jnp.where(
            (a_row[:, None, None] == c_rows) & (b_col[None, :, None] == c_cols), slots + 1, 0
        ),
        axis=2,
    )
    meets = (a_inner[:, None] == b_inner[None, :]) & (a_code >= 0)[:, None] & (slot > 0)
    position = jnp.arange(b_code.shape[0], dtype=jnp.int32)
    key = position[None, :] * 32 + slot - 1
    first = jnp.min(jnp.where(meets, key, 1 << 20), axis=1)
    last = jnp.max(jnp.where(meets, key, -1), axis=1)
    one = last >= 0
    two = one & (first != last)
    keys = jnp.concatenate([last, first])
    there = jnp.concatenate([one, two])
    a_slot = jnp.tile(jnp.arange(a_code.shape[0], dtype=jnp.int32), 2)
    total = keys.shape[0]
    entry = jnp.where(there, a_slot * 8192 + keys, 0)
    spots = jnp.arange(total, dtype=jnp.int32)
    rank = jnp.sum((there[None, :] & (spots[None, :] < spots[:, None])).astype(jnp.int32), axis=1)
    picked = there[:, None] & (rank[:, None] == spots[None, :])
    listed = jnp.sum(jnp.where(picked, entry[:, None], 0), axis=0)
    count = jnp.sum(there.astype(jnp.int32))
    return jnp.where(spots < count, listed, kept), count[None]


def product_kernel(
    list_ref, count_ref, a_ref, b_ref, out_ref, a_buffer, b_buffer, total, a_sem, b_sem
):
    kept = out_ref.shape[0]
    batches = (count_ref[0] + BATCH - 1) // BATCH

    def fetch(batch):
        spot = batch % DEPTH
        for n in range(BATCH):
            entry = list_ref[batch * BATCH + n]
            pltpu.make_async_copy(
                a_ref.at[entry // 8192], a_buffer.at[spot, n], a_sem.at[spot]
            ).start()
            pltpu.make_async_copy(
                b_ref.at[(entry // 32) % 256], b_buffer.at[spot, n], b_sem.at[spot]
            ).start()

    def prefetch(batch, carry):
        fetch(batch)
        return carry

    lax.fori_loop(0, jnp.minimum(batches, DEPTH), prefetch, 0)
    total[...] = jnp.zeros_like(total)

    def work(batch, carry):
        spot = batch % DEPTH
        pltpu.make_async_copy(a_buffer.at[spot], a_buffer.at[spot], a_sem.at[spot]).wait()
        pltpu.make_async_copy(b_buffer.at[spot], b_buffer.at[spot], b_sem.at[spot]).wait()
        products = [
            jnp.dot(
                a_buffer[spot, n], b_buffer[spot, n], preferred_element_type=jnp.float32
            )
            for n in range(BATCH)
        ]
        for n in range(BATCH):
            slot = list_ref[batch * BATCH + n] % 32
            total[slot] += products[n]

        @pl.when(batch + DEPTH < batches)
        def _():
            fetch(batch + DEPTH)

        return carry

    lax.fori_loop(0, batches, work, 0)
    out_ref[...] = total[0:kept].astype(out_ref.dtype)


def partial_product(listed, count, a_all, b_all, kept):
    smem = pl.BlockSpec(memory_space=pltpu.SMEM)
    anywhere = pl.BlockSpec(memory_space=pl.ANY)
    return pl.pallas_call(
        product_kernel,
        out_shape=jax.ShapeDtypeStruct((kept, BLOCK, BLOCK), jnp.bfloat16),
        in_specs=[smem, smem, anywhere, anywhere],
        out_specs=pl.BlockSpec(memory_space=pltpu.VMEM),
        scratch_shapes=[
            pltpu.VMEM((DEPTH, BATCH, BLOCK, BLOCK), jnp.bfloat16),
            pltpu.VMEM((DEPTH, BATCH, BLOCK, BLOCK), jnp.bfloat16),
            pltpu.VMEM((kept + 1, BLOCK, BLOCK), jnp.float32),
            pltpu.SemaphoreType.DMA((DEPTH,)),
            pltpu.SemaphoreType.DMA((DEPTH,)),
        ],
        compiler_params=pltpu.CompilerParams(vmem_limit_bytes=60 << 20),
        name="partial_product",
    )(listed, count, a_all, b_all)


A_CHUNKS = ((0, 6, 1), (6, 6, 1), (12, 6, -1), (18, 6, -1))
B_CHUNKS = ((0, 4, 1, True), (4, 4, -1, True), (8, 4, 1, False), (12, 4, -1, False))


def gather_kernel(a_ref, b_ref, m_ref, a_all, b_all, a_marks, b_marks, send_sem, recv_sem, own_sem):
    col, row = lax.axis_index("col"), lax.axis_index("row")
    a_ring, b_ring = lax.axis_size("col"), lax.axis_size("row") // 2
    plane, spot = row // b_ring, row % b_ring
    partner = row + b_ring - 2 * b_ring * plane

    def a_peer(way):
        return {"col": lax.rem(col + way + a_ring, a_ring)}

    def b_peer(way):
        return {"row": plane * b_ring + lax.rem(spot + way + b_ring, b_ring)}

    barrier = pltpu.get_barrier_semaphore()
    peers = (a_peer(1), a_peer(-1), b_peer(1), b_peer(-1), {"row": partner})
    for peer in peers:
        pl.semaphore_signal(barrier, inc=1, device_id=peer, device_id_type=MESH)
    pl.semaphore_wait(barrier, len(peers))

    numbers = {}
    sent = []

    def number(name):
        return numbers.setdefault(name, len(numbers))

    def send(name, source, target, peer):
        at = number(name)
        copy = pltpu.make_async_remote_copy(
            src_ref=source,
            dst_ref=target,
            send_sem=send_sem.at[at],
            recv_sem=recv_sem.at[at],
            device_id=peer,
            device_id_type=MESH,
        )
        copy.start()
        sent.append(copy)

    def arrive(name, target, peer):
        at = number(name)
        pltpu.make_async_remote_copy(
            src_ref=target,
            dst_ref=target,
            send_sem=send_sem.at[at],
            recv_sem=recv_sem.at[at],
            device_id=peer,
            device_id_type=MESH,
        ).wait_recv()

    a_pieces = [("marks", lambda o: a_marks.at[o], m_ref, 1, 0.0)]
    for n, (start, size, way) in enumerate(A_CHUNKS):
        a_pieces.append(
            (
                f"a{n}",
                lambda o, start=start, size=size: a_all.at[o, pl.ds(start, size)],
                a_ref.at[pl.ds(start, size)],
                way,
                size,
            )
        )
    b_pieces = [("marks", lambda o: b_marks.at[o], m_ref, 1, 0.0, False)]
    for n, (start, size, way, later) in enumerate(B_CHUNKS):
        b_pieces.append(
            (
                f"b{n}",
                lambda o, start=start, size=size: b_all.at[o, pl.ds(start, size)],
                b_ref.at[pl.ds(start, size)],
                way,
                size,
                later,
            )
        )

    events = []

    def forward_a(piece, way, step, origin, source):
        last = a_ring // 2
        if step < last or (step == last and piece[3] == way):
            send(("a", piece[0], way, step), source, piece[1](origin), a_peer(way))

    def forward_b(piece, way, step, side, origin, source):
        last = b_ring // 2
        if step < last or (step == last and piece[3] == way):
            send(("b", piece[0], way, step, side), source, piece[1](origin), b_peer(way))

    def b_origin(side, place):
        return (plane if side == "own" else 1 - plane) * b_ring + place

    for piece in b_pieces:
        if not piece[5]:
            send(("x", piece[0], 0, 0), piece[2], piece[1](row), {"row": partner})
    own = [
        pltpu.make_async_copy(a_ref, a_all.at[col], own_sem.at[0]),
        pltpu.make_async_copy(b_ref, b_all.at[row], own_sem.at[1]),
        pltpu.make_async_copy(m_ref, a_marks.at[col], own_sem.at[2]),
        pltpu.make_async_copy(m_ref, b_marks.at[row], own_sem.at[3]),
    ]
    for way in (1, -1):
        forward_a(a_pieces[0], way, 1, col, a_pieces[0][2])
        forward_b(b_pieces[0], way, 1, "own", row, b_pieces[0][2])
    for rank in range(len(A_CHUNKS)):
        for way in (1, -1):
            piece = a_pieces[1:][rank if way == 1 else -1 - rank]
            forward_a(piece, way, 1, col, piece[2])
    for rank in range(len(B_CHUNKS)):
        for way in (1, -1):
            piece = b_pieces[1:][rank if way == 1 else -1 - rank]
            forward_b(piece, way, 1, "own", row, piece[2])
    for piece in b_pieces:
        if piece[5]:
            send(("x", piece[0], 0, 0), piece[2], piece[1](row), {"row": partner})
    for copy in own:
        copy.start()

    a_step = sum(piece[4] for piece in a_pieces)
    b_step = sum(piece[4] * (1 if piece[5] else 2) for piece in b_pieces)

    def arrive_a(piece, way, step):
        origin = lax.rem(col - way * step + a_ring, a_ring)
        place = piece[1](origin)
        arrive(("a", piece[0], way, step), place, a_peer(way))
        forward_a(piece, way, step + 1, origin, place)

    def arrive_b(piece, way, step, side):
        origin = b_origin(side, lax.rem(spot - way * step + b_ring, b_ring))
        place = piece[1](origin)
        arrive(("b", piece[0], way, step, side), place, b_peer(way))
        forward_b(piece, way, step + 1, side, origin, place)
        if piece[5]:
            send(("x", piece[0], way, step), place, place, {"row": partner})

    def arrive_x(piece, way, step):
        origin = b_origin("far", lax.rem(spot - way * step + b_ring, b_ring))
        place = piece[1](origin)
        arrive(("x", piece[0], way, step), place, {"row": partner})
        if step == 0 and not piece[5]:
            for on in (1, -1):
                forward_b(piece, on, 1, "far", origin, place)

    for way in (1, -1):
        for step in range(1, a_ring // 2 + 1):
            done = (step - 1) * a_step
            for piece in a_pieces[:1] + a_pieces[1:][::way]:
                if step < a_ring // 2 or piece[3] == way:
                    done += piece[4]
                    events.append((2 * done, functools.partial(arrive_a, piece, way, step)))
        for step in range(1, b_ring // 2 + 1):
            done = (step - 1) * b_step
            for side in ("own", "far"):
                for piece in b_pieces[:1] + b_pieces[1:][::way]:
                    if side == "far" and piece[5]:
                        continue
                    if step < b_ring // 2 or piece[3] == way:
                        done += piece[4]
                        events.append(
                            (2 * done, functools.partial(arrive_b, piece, way, step, side))
                        )
                        if piece[5]:
                            events.append(
                                (2 * done + 40, functools.partial(arrive_x, piece, way, step))
                            )
    x_done = 0
    for piece in b_pieces:
        if not piece[5]:
            x_done += piece[4]
            events.append((3 * x_done, functools.partial(arrive_x, piece, 0, 0)))
    for piece in b_pieces:
        if piece[5]:
            events.append((60, functools.partial(arrive_x, piece, 0, 0)))
    for _, event in sorted(events, key=lambda e: e[0]):
        event()
    for copy in own:
        copy.wait()
    for copy in sent:
        copy.wait_send()
    assert len(numbers) <= SEMAPHORES


def gathered(a_own, b_own, marks):
    anywhere = pl.BlockSpec(memory_space=pl.ANY)
    cols, rows = lax.axis_size("col"), lax.axis_size("row")
    return pl.pallas_call(
        gather_kernel,
        out_shape=(
            jax.ShapeDtypeStruct((cols,) + a_own.shape, a_own.dtype),
            jax.ShapeDtypeStruct((rows,) + b_own.shape, b_own.dtype),
            jax.ShapeDtypeStruct((cols,) + marks.shape, marks.dtype),
            jax.ShapeDtypeStruct((rows,) + marks.shape, marks.dtype),
        ),
        in_specs=[anywhere] * 3,
        out_specs=(anywhere,) * 4,
        scratch_shapes=[
            pltpu.SemaphoreType.DMA((SEMAPHORES,)),
            pltpu.SemaphoreType.DMA((SEMAPHORES,)),
            pltpu.SemaphoreType.DMA((4,)),
        ],
        compiler_params=pltpu.CompilerParams(
            collective_id=0, has_side_effects=True, vmem_limit_bytes=60 << 20
        ),
        name="gather_blocks",
    )(a_own, b_own, marks)


def layer_sum_kernel(partial_ref, out_ref, from_sibling, pair, from_far, send_sem, recv_sem):
    layer = lax.axis_index("layer")
    share = out_ref.shape[0]
    sibling = {"layer": layer + 1 - 2 * lax.rem(layer, 2)}
    far = {"layer": lax.rem(layer + 2, 4)}
    barrier = pltpu.get_barrier_semaphore()
    for peer in (sibling, far):
        pl.semaphore_signal(barrier, inc=1, device_id=peer, device_id_type=MESH)
    pl.semaphore_wait(barrier, 2)

    def group(ref, owner):
        return ref.at[pl.ds(owner * share, share)]

    def copy(n, source, target, peer):
        return pltpu.make_async_remote_copy(
            src_ref=source,
            dst_ref=target,
            send_sem=send_sem.at[n],
            recv_sem=recv_sem.at[n],
            device_id=peer,
            device_id_type=MESH,
        )

    on = copy(0, group(partial_ref, lax.rem(sibling["layer"] + 2, 4)), from_sibling.at[0], sibling)
    kept = copy(1, group(partial_ref, sibling["layer"]), from_sibling.at[1], sibling)
    on.start()
    kept.start()
    on.wait_recv()
    pair[...] = (
        group(partial_ref, far["layer"])[...].astype(jnp.float32)
        + from_sibling[0].astype(jnp.float32)
    ).astype(pair.dtype)
    across = copy(2, pair, from_far, far)
    across.start()
    kept.wait_recv()
    across.wait_recv()
    out_ref[...] = (
        group(partial_ref, layer)[...].astype(jnp.float32)
        + from_sibling[1].astype(jnp.float32)
        + from_far[...].astype(jnp.float32)
    ).astype(out_ref.dtype)
    on.wait_send()
    kept.wait_send()
    across.wait_send()


def layer_sum(partial):
    share = (partial.shape[0] // lax.axis_size("layer"),) + partial.shape[1:]
    vmem = pl.BlockSpec(memory_space=pltpu.VMEM)
    return pl.pallas_call(
        layer_sum_kernel,
        out_shape=jax.ShapeDtypeStruct(share, partial.dtype),
        in_specs=[vmem],
        out_specs=vmem,
        scratch_shapes=[
            pltpu.VMEM((2,) + share, partial.dtype),
            pltpu.VMEM(share, partial.dtype),
            pltpu.VMEM(share, partial.dtype),
            pltpu.SemaphoreType.DMA((3,)),
            pltpu.SemaphoreType.DMA((3,)),
        ],
        compiler_params=pltpu.CompilerParams(
            collective_id=1, has_side_effects=True, vmem_limit_bytes=60 << 20
        ),
        name="layer_sum",
    )(partial)


def shards(a_blocks, a_index, a_send, a_count, b_blocks, b_index, b_send, b_count, c_index):
    a_own, b_own = a_blocks[0, 0, 0], b_blocks[0, 0, 0]
    a_rows, a_cols = a_index[0, 0, 0, 0], a_index[0, 0, 0, 1]
    b_rows, b_cols = b_index[0, 0, 0, 0], b_index[0, 0, 0, 1]
    a_live = live_slots(a_send[0, 0, 0], a_count[0, 0, 0], a_own.shape[0])
    b_live = live_slots(b_send[0, 0, 0], b_count[0, 0, 0], b_own.shape[0])
    a_code = jnp.where(a_live, (a_cols // 32 * 8 + a_cols % 8) * 32 + a_rows // 16, -1)
    b_code = jnp.where(b_live, (b_rows // 32 * 8 + b_rows % 8) * 64 + b_cols // 8, -1)
    codes = jnp.concatenate([a_code, b_code, jnp.full((88,), -1, jnp.int32)])
    marks = jnp.broadcast_to(codes, (8, 128))
    a_all, b_all, a_marks, b_marks = gathered(a_own, b_own, marks)
    a_held, b_held = a_own.shape[0], b_own.shape[0]
    a_code = a_marks[:, 0, :a_held].reshape(-1)
    b_code = b_marks[:, 0, a_held : a_held + b_held].reshape(-1)
    a_all = a_all.reshape(-1, BLOCK, BLOCK)
    b_all = b_all.reshape(-1, BLOCK, BLOCK)
    listed, count = product_list(a_code, b_code, c_index[0, 0])
    partial = partial_product(listed, count, a_all, b_all, c_index.shape[3])
    return layer_sum(partial)[None, None]


def solution(mesh):
    in_specs = (
        P("row", "col", "layer", None, None, None),
        P("row", "col", "layer", None, None),
        P("row", "col", "layer", None, None),
        P("row", "col", "layer", None),
        P("row", "col", "layer", None, None, None),
        P("row", "col", "layer", None, None),
        P("row", "col", "layer", None, None),
        P("row", "col", "layer", None),
        P("row", "col", None, None),
    )
    out_specs = P("row", "col", "layer", None, None)
    return jax.shard_map(shards, mesh=mesh, in_specs=in_specs, out_specs=out_specs, check_vma=False)
```

```python
import functools

import jax
import jax.numpy as jnp
from jax import lax
from jax.experimental import pallas as pl
from jax.experimental.pallas import tpu as pltpu
from jax.sharding import PartitionSpec as P

BLOCK = 128
BATCH = 8
DEPTH = 4
SEMAPHORES = 128
PIECES = 3
MESH = pl.DeviceIdType.MESH


def own_marks(col, row, a_index, a_send, a_count, b_index, b_send, b_count):
    shape = (8, 128)
    place = lax.broadcasted_iota(jnp.int32, shape, 0) * 128 + lax.broadcasted_iota(
        jnp.int32, shape, 1
    )
    marks = jnp.zeros(shape, jnp.int32)
    for base, first, index, inner_at, send, count in (
        (0, col * a_index.shape[4], a_index, 1, a_send, a_count),
        (512, row * b_index.shape[4], b_index, 0, b_send, b_count),
    ):
        spread = 16 if inner_at else 8
        live = place < 0
        for d in range(send.shape[1]):
            for m in range(send.shape[0]):
                slot = jnp.where(m < count[0, 0, 0, d], base + first + send[m, d], -1)
                live = live | (place == slot)
        inner = jnp.zeros(shape, jnp.int32)
        for slot in range(index.shape[4]):
            k = index[0, 0, 0, inner_at, slot]
            other = index[0, 0, 0, 1 - inner_at, slot]
            inner = jnp.where(
                place == base + first + slot, lax.div(k, 32) * 8 + lax.rem(k, 8) + 1, inner
            )
            marks = jnp.where(place == base + 256 + first + slot, lax.div(other, spread), marks)
        marks = jnp.where(live, inner, marks)
    return marks


def product_list(a_marks, b_marks, c_index):
    kept = c_index.shape[3]
    a_sum = a_marks[0]
    for n in range(1, a_marks.shape[0]):
        a_sum = a_sum + a_marks[n]
    b_sum = b_marks[0]
    for n in range(1, b_marks.shape[0]):
        b_sum = b_sum + b_marks[n]
    square = (128, 128)
    sub = lax.broadcasted_iota(jnp.int32, square, 0)
    lane = lax.broadcasted_iota(jnp.int32, square, 1)
    sub_f, lane_f = sub.astype(jnp.float32), lane.astype(jnp.float32)
    eye = sub == lane

    def column(values):
        return jnp.sum(jnp.where(eye, values, 0.0), axis=1, keepdims=True)

    def line(values):
        return jnp.sum(jnp.where(eye, values, 0.0), axis=0, keepdims=True)

    a_f, b_f = a_sum.astype(jnp.float32), b_sum.astype(jnp.float32)
    c_code = [
        (lax.div(c_index[0, 0, 0, m], 16) * 64 + lax.div(c_index[0, 0, 1, m], 8)).astype(
            jnp.float32
        )
        for m in range(kept)
    ]
    entries = []
    for i in range(2):
        a_inner = column(a_f[i : i + 1])
        a_row = column(a_f[2 + i : 3 + i])
        first = jnp.full((128, 1), 65536.0, jnp.float32)
        last = jnp.full((128, 1), -1.0, jnp.float32)
        for j in range(2):
            b_inner, b_col = b_f[4 + j : 5 + j], b_f[6 + j : 7 + j]
            position = a_row * 64.0 + b_col
            slot = jnp.full(square, -1.0, jnp.float32)
            for m in range(kept):
                slot = jnp.where(position == c_code[m], float(m), slot)
            meets = (a_inner == b_inner) & (a_inner > 0.0) & (slot >= 0.0)
            key = (lane_f + 128.0 * j) * 32.0 + slot
            first = jnp.minimum(
                first, jnp.min(jnp.where(meets, key, 65536.0), axis=1, keepdims=True)
            )
            last = jnp.maximum(last, jnp.max(jnp.where(meets, key, -1.0), axis=1, keepdims=True))
        entries.append((i, last, last >= 0.0))
        entries.append((i, first, (last >= 0.0) & (first != last)))
    sub_1 = sub_f[:, :1]
    columns = []
    for n, (i, key, there) in enumerate(entries):
        slot = key - 32.0 * jnp.floor(key * (1.0 / 32.0))
        order = jnp.where(there, slot * 512.0 + (sub_1 + 128.0 * n), 65536.0)
        value = jnp.where(there, (sub_1 + 128.0 * i) * 8192.0 + key, 0.0)
        columns.append((there, slot, order, value))
    lines = [line(order) for _, _, order, _ in columns]
    listed = [jnp.zeros((1, 128), jnp.float32) for _ in range(3)]
    starts = jnp.zeros((1, 128), jnp.float32)
    for there, slot, order, value in columns:
        rank = jnp.zeros((128, 1), jnp.float32)
        for other in lines:
            rank = rank + jnp.sum(jnp.where(other < order, 1.0, 0.0), axis=1, keepdims=True)
        rank = jnp.where(there, rank, -1.0)
        for n in range(3):
            listed[n] = listed[n] + jnp.sum(
                jnp.where(rank == lane_f + 128.0 * n, value, 0.0), axis=0, keepdims=True
            )
        starts = starts + jnp.sum(
            jnp.where(there & (slot < lane_f), 1.0, 0.0), axis=0, keepdims=True
        )
    count = starts[:, kept : kept + 1]
    rows = [
        jnp.where(lane_f[:1] + 128.0 * n < count, listed[n], float(kept)) for n in range(3)
    ] + [jnp.broadcast_to(count, (1, 128)), starts]
    rows = jnp.concatenate(rows + [jnp.zeros((3, 128), jnp.float32)], axis=0)
    return rows.astype(jnp.int32)


def product_kernel(
    list_ref, a_ref, b_ref, out_ref, a_buffer, b_buffer, total, a_sem, b_sem
):
    kept = out_ref.shape[0]
    batches = (list_ref[3, 0] + BATCH - 1) // BATCH

    def listed(at):
        return list_ref[lax.shift_right_logical(at, 7), at & 127]

    def fetch(batch):
        spot = batch & (DEPTH - 1)
        for n in range(BATCH):
            entry = listed(batch * BATCH + n)
            pltpu.make_async_copy(
                a_ref.at[lax.shift_right_logical(entry, 13)], a_buffer.at[spot, n], a_sem.at[spot]
            ).start()
            pltpu.make_async_copy(
                b_ref.at[lax.shift_right_logical(entry, 5) & 255], b_buffer.at[spot, n], b_sem.at[spot]
            ).start()

    def prefetch(batch, carry):
        fetch(batch)
        return carry

    lax.fori_loop(0, jnp.minimum(batches, DEPTH), prefetch, 0)
    total[...] = jnp.zeros_like(total)

    def work(batch, carry):
        spot = batch & (DEPTH - 1)
        pltpu.make_async_copy(a_buffer.at[spot], a_buffer.at[spot], a_sem.at[spot]).wait()
        pltpu.make_async_copy(b_buffer.at[spot], b_buffer.at[spot], b_sem.at[spot]).wait()
        products = [
            jnp.dot(
                a_buffer[spot, n], b_buffer[spot, n], preferred_element_type=jnp.float32
            )
            for n in range(BATCH)
        ]
        for n in range(BATCH):
            slot = listed(batch * BATCH + n) & 31
            total[slot] += products[n]

        @pl.when(batch + DEPTH < batches)
        def _():
            fetch(batch + DEPTH)

        return carry

    lax.fori_loop(0, batches, work, 0)
    out_ref[...] = total[0:kept].astype(out_ref.dtype)


def partial_product(listed, a_all, b_all, kept):
    smem = pl.BlockSpec(memory_space=pltpu.SMEM)
    anywhere = pl.BlockSpec(memory_space=pl.ANY)
    return pl.pallas_call(
        product_kernel,
        out_shape=jax.ShapeDtypeStruct((kept, BLOCK, BLOCK), jnp.bfloat16),
        in_specs=[smem, anywhere, anywhere],
        out_specs=pl.BlockSpec(memory_space=pltpu.VMEM),
        scratch_shapes=[
            pltpu.VMEM((DEPTH, BATCH, BLOCK, BLOCK), jnp.bfloat16),
            pltpu.VMEM((DEPTH, BATCH, BLOCK, BLOCK), jnp.bfloat16),
            pltpu.VMEM((kept + 1, BLOCK, BLOCK), jnp.float32),
            pltpu.SemaphoreType.DMA((DEPTH,)),
            pltpu.SemaphoreType.DMA((DEPTH,)),
        ],
        compiler_params=pltpu.CompilerParams(vmem_limit_bytes=60 << 20),
        name="partial_product",
    )(listed, a_all, b_all)


A_CHUNKS = ((0, 6, 1), (6, 6, 1), (12, 6, -1), (18, 6, -1))
B_CHUNKS = ((0, 5, 1, True), (5, 4, -1, True), (9, 3, 1, False), (12, 4, -1, False))


def gather_kernel(
    a_ref,
    b_ref,
    *rest,
):
    tables, (a_all, b_all, list_ref, m_ref, a_marks, b_marks) = rest[:7], rest[7:13]
    send_sem, recv_sem, own_sem = rest[13:16]
    scalars = rest[16:]
    loads = [
        pltpu.make_async_copy(table, held, own_sem.at[2 + n])
        for n, (table, held) in enumerate(zip(tables, scalars))
    ]
    for load in loads:
        load.start()
    a_index, a_send, a_count, b_index, b_send, b_count, c_index = scalars
    col, row = lax.axis_index("col"), lax.axis_index("row")
    a_ring, b_ring = lax.axis_size("col"), lax.axis_size("row") // 2
    plane, spot = row // b_ring, row % b_ring
    partner = row + b_ring - 2 * b_ring * plane

    def a_peer(way):
        return {"col": lax.rem(col + way + a_ring, a_ring)}

    def b_peer(way):
        return {"row": plane * b_ring + lax.rem(spot + way + b_ring, b_ring)}

    barrier = pltpu.get_barrier_semaphore()
    peers = (a_peer(1), a_peer(-1), b_peer(1), b_peer(-1), {"row": partner})
    for peer in peers:
        pl.semaphore_signal(barrier, inc=1, device_id=peer, device_id_type=MESH)
    pl.semaphore_wait(barrier, len(peers))

    numbers = {}
    sent = []

    def number(name):
        return numbers.setdefault(name, len(numbers))

    def send(name, source, target, peer):
        at = number(name)
        copy = pltpu.make_async_remote_copy(
            src_ref=source,
            dst_ref=target,
            send_sem=send_sem.at[at],
            recv_sem=recv_sem.at[at],
            device_id=peer,
            device_id_type=MESH,
        )
        copy.start()
        sent.append(copy)

    def arrive(name, target, peer):
        at = number(name)
        pltpu.make_async_remote_copy(
            src_ref=target,
            dst_ref=target,
            send_sem=send_sem.at[at],
            recv_sem=recv_sem.at[at],
            device_id=peer,
            device_id_type=MESH,
        ).wait_recv()

    a_pieces = [("marks", lambda o: a_marks.at[o], m_ref, 1, 0.0)]
    for n, (start, size, way) in enumerate(A_CHUNKS):
        a_pieces.append(
            (
                f"a{n}",
                lambda o, start=start, size=size: a_all.at[o, pl.ds(start, size)],
                a_ref.at[pl.ds(start, size)],
                way,
                size,
            )
        )
    b_pieces = [("marks", lambda o: b_marks.at[o], m_ref, 1, 0.0, False)]
    for n, (start, size, way, later) in enumerate(B_CHUNKS):
        b_pieces.append(
            (
                f"b{n}",
                lambda o, start=start, size=size: b_all.at[o, pl.ds(start, size)],
                b_ref.at[pl.ds(start, size)],
                way,
                size,
                later,
            )
        )

    events = []

    def forward_a(piece, way, step, origin, source):
        last = a_ring // 2
        if step < last or (step == last and piece[3] == way):
            send(("a", piece[0], way, step), source, piece[1](origin), a_peer(way))

    def forward_b(piece, way, step, side, origin, source):
        last = b_ring // 2
        if step < last or (step == last and piece[3] == way):
            send(("b", piece[0], way, step, side), source, piece[1](origin), b_peer(way))

    def b_origin(side, place):
        return (plane if side == "own" else 1 - plane) * b_ring + place

    for piece in b_pieces[1:]:
        if not piece[5]:
            send(("x", piece[0], 0, 0), piece[2], piece[1](row), {"row": partner})
    for rank in range(len(A_CHUNKS)):
        for way in (1, -1):
            piece = a_pieces[1:][rank if way == 1 else -1 - rank]
            forward_a(piece, way, 1, col, piece[2])
    for rank in range(len(B_CHUNKS)):
        for way in (1, -1):
            piece = b_pieces[1:][rank if way == 1 else -1 - rank]
            forward_b(piece, way, 1, "own", row, piece[2])
    for piece in b_pieces[1:]:
        if piece[5]:
            send(("x", piece[0], 0, 0), piece[2], piece[1](row), {"row": partner})
    for load in loads:
        load.wait()
    m_ref[...] = own_marks(
        col, row, a_index, a_send.at[0, 0, :, 0], a_count, b_index, b_send.at[0, 0, 0], b_count
    )
    send(("x", "marks", 0, 0), m_ref, b_marks.at[row], {"row": partner})
    for way in (1, -1):
        forward_a(a_pieces[0], way, 1, col, m_ref)
        forward_b(b_pieces[0], way, 1, "own", row, m_ref)
    own = [
        pltpu.make_async_copy(a_ref, a_all.at[col], own_sem.at[0]),
        pltpu.make_async_copy(b_ref, b_all.at[row], own_sem.at[1]),
    ]
    for copy in own:
        copy.start()
    a_marks[col] = m_ref[...]
    b_marks[row] = m_ref[...]

    a_step = sum(piece[4] for piece in a_pieces)
    b_step = sum(piece[4] * (1 if piece[5] else 2) for piece in b_pieces)

    def arrive_a(piece, way, step):
        origin = lax.rem(col - way * step + a_ring, a_ring)
        place = piece[1](origin)
        arrive(("a", piece[0], way, step), place, a_peer(way))
        forward_a(piece, way, step + 1, origin, place)

    def arrive_b(piece, way, step, side):
        origin = b_origin(side, lax.rem(spot - way * step + b_ring, b_ring))
        place = piece[1](origin)
        arrive(("b", piece[0], way, step, side), place, b_peer(way))
        forward_b(piece, way, step + 1, side, origin, place)
        if piece[5]:
            send(("x", piece[0], way, step), place, place, {"row": partner})

    def arrive_x(piece, way, step):
        origin = b_origin("far", lax.rem(spot - way * step + b_ring, b_ring))
        place = piece[1](origin)
        arrive(("x", piece[0], way, step), place, {"row": partner})
        if step == 0 and not piece[5]:
            for on in (1, -1):
                forward_b(piece, on, 1, "far", origin, place)

    def expect(time, event, *about):
        events.append((time, functools.partial(event, *about)))

    for way in (1, -1):
        for step in range(1, a_ring // 2 + 1):
            done = (step - 1) * a_step
            if step < a_ring // 2 or a_pieces[0][3] == way:
                expect(2 * done + a_step, arrive_a, a_pieces[0], way, step)
            for piece in a_pieces[1:][::way]:
                if step < a_ring // 2 or piece[3] == way:
                    done += piece[4]
                    expect(2 * done, arrive_a, piece, way, step)
        for step in range(1, b_ring // 2 + 1):
            done = (step - 1) * b_step
            if step < b_ring // 2 or b_pieces[0][3] == way:
                expect(2 * done + a_step + 0.2, arrive_b, b_pieces[0], way, step, "own")
                expect(2 * done + a_step + 0.4, arrive_b, b_pieces[0], way, step, "far")
            for side in ("own", "far"):
                for piece in b_pieces[1:][::way]:
                    if side == "far" and piece[5]:
                        continue
                    if step < b_ring // 2 or piece[3] == way:
                        done += piece[4]
                        expect(2 * done, arrive_b, piece, way, step, side)
                        if piece[5]:
                            expect(2 * done + 40, arrive_x, piece, way, step)
    x_done = 0
    expect(a_step, arrive_x, b_pieces[0], 0, 0)
    for piece in b_pieces[1:]:
        if not piece[5]:
            x_done += piece[4]
            expect(3 * x_done, arrive_x, piece, 0, 0)
        else:
            expect(60, arrive_x, piece, 0, 0)

    def write_list():
        list_ref[...] = product_list(a_marks, b_marks, c_index)

    expect(2 * (max(a_ring // 2 * a_step, b_ring // 2 * b_step) - min(a_step, b_step)) + a_step + 0.6, write_list)
    for _, event in sorted(events, key=lambda e: e[0]):
        event()
    for copy in own:
        copy.wait()
    for copy in sent:
        copy.wait_send()
    assert len(numbers) <= SEMAPHORES


def gathered(a_own, b_own, a_index, a_send, a_count, b_index, b_send, b_count, c_index):
    anywhere = pl.BlockSpec(memory_space=pl.ANY)
    tables = (a_index, a_send, a_count, b_index, b_send, b_count, c_index)
    cols, rows = lax.axis_size("col"), lax.axis_size("row")
    return pl.pallas_call(
        gather_kernel,
        out_shape=(
            jax.ShapeDtypeStruct((cols,) + a_own.shape, a_own.dtype),
            jax.ShapeDtypeStruct((rows,) + b_own.shape, b_own.dtype),
            jax.ShapeDtypeStruct((8, 128), jnp.int32),
        ),
        in_specs=[anywhere] * (2 + len(tables)),
        out_specs=(anywhere, anywhere, pl.BlockSpec(memory_space=pltpu.VMEM)),
        scratch_shapes=[
            pltpu.VMEM((8, 128), jnp.int32),
            pltpu.VMEM((cols, 8, 128), jnp.int32),
            pltpu.VMEM((rows, 8, 128), jnp.int32),
            pltpu.SemaphoreType.DMA((SEMAPHORES,)),
            pltpu.SemaphoreType.DMA((SEMAPHORES,)),
            pltpu.SemaphoreType.DMA((2 + len(tables),)),
        ]
        + [pltpu.SMEM(table.shape, table.dtype) for table in tables],
        compiler_params=pltpu.CompilerParams(
            collective_id=0, has_side_effects=True, vmem_limit_bytes=60 << 20
        ),
        name="gather_blocks",
    )(a_own, b_own, *tables)


def layer_sum_kernel(
    partial_ref, out_ref, mine, from_sibling, pair, from_far, send_sem, recv_sem, own_sem
):
    layer = lax.axis_index("layer")
    share = out_ref.shape[0]
    piece = share // PIECES
    sibling = {"layer": layer + 1 - 2 * lax.rem(layer, 2)}
    far = {"layer": lax.rem(layer + 2, 4)}
    loads = [
        pltpu.make_async_copy(
            partial_ref.at[pl.ds(owner * share, share)], mine.at[n], own_sem.at[n]
        )
        for n, owner in enumerate((far["layer"], layer))
    ]
    for load in loads:
        load.start()
    barrier = pltpu.get_barrier_semaphore()
    for peer in (sibling, far):
        pl.semaphore_signal(barrier, inc=1, device_id=peer, device_id_type=MESH)
    pl.semaphore_wait(barrier, 2)

    def copy(n, source, target, peer):
        return pltpu.make_async_remote_copy(
            src_ref=source,
            dst_ref=target,
            send_sem=send_sem.at[n],
            recv_sem=recv_sem.at[n],
            device_id=peer,
            device_id_type=MESH,
        )

    on, across = [], []
    for n, owner in enumerate((lax.rem(sibling["layer"] + 2, 4), sibling["layer"])):
        for p in range(PIECES):
            on.append(
                copy(
                    n * PIECES + p,
                    partial_ref.at[pl.ds(owner * share + p * piece, piece)],
                    from_sibling.at[n, pl.ds(p * piece, piece)],
                    sibling,
                )
            )
            on[-1].start()
    loads[0].wait()
    for p in range(PIECES):
        at = pl.ds(p * piece, piece)
        on[p].wait_recv()
        pair[at] = (
            mine[0, at].astype(jnp.float32) + from_sibling[0, at].astype(jnp.float32)
        ).astype(pair.dtype)
        across.append(copy(2 * PIECES + p, pair.at[at], from_far.at[at], far))
        across[-1].start()
    loads[1].wait()
    for p in range(PIECES):
        on[PIECES + p].wait_recv()
    for p in range(PIECES):
        at = pl.ds(p * piece, piece)
        across[p].wait_recv()
        out_ref[at] = (
            mine[1, at].astype(jnp.float32)
            + from_sibling[1, at].astype(jnp.float32)
            + from_far[at].astype(jnp.float32)
        ).astype(out_ref.dtype)
    for sent in on + across:
        sent.wait_send()


def layer_sum(partial):
    share = (partial.shape[0] // lax.axis_size("layer"),) + partial.shape[1:]
    return pl.pallas_call(
        layer_sum_kernel,
        out_shape=jax.ShapeDtypeStruct(share, partial.dtype),
        in_specs=[pl.BlockSpec(memory_space=pl.ANY)],
        out_specs=pl.BlockSpec(memory_space=pltpu.VMEM),
        scratch_shapes=[
            pltpu.VMEM((2,) + share, partial.dtype),
            pltpu.VMEM((2,) + share, partial.dtype),
            pltpu.VMEM(share, partial.dtype),
            pltpu.VMEM(share, partial.dtype),
            pltpu.SemaphoreType.DMA((3 * PIECES,)),
            pltpu.SemaphoreType.DMA((3 * PIECES,)),
            pltpu.SemaphoreType.DMA((2,)),
        ],
        compiler_params=pltpu.CompilerParams(
            collective_id=1, has_side_effects=True, vmem_limit_bytes=60 << 20
        ),
        name="layer_sum",
    )(partial)


def shards(a_blocks, a_index, a_send, a_count, b_blocks, b_index, b_send, b_count, c_index):
    a_all, b_all, listed = gathered(
        a_blocks[0, 0, 0],
        b_blocks[0, 0, 0],
        a_index,
        jnp.transpose(a_send, (0, 1, 4, 2, 3)),
        a_count,
        b_index,
        jnp.transpose(b_send, (0, 1, 2, 4, 3)),
        b_count,
        c_index,
    )
    a_all = a_all.reshape(-1, BLOCK, BLOCK)
    b_all = b_all.reshape(-1, BLOCK, BLOCK)
    partial = partial_product(listed, a_all, b_all, c_index.shape[3])
    return layer_sum(partial)[None, None]


def solution(mesh):
    in_specs = (
        P("row", "col", "layer", None, None, None),
        P("row", "col", "layer", None, None),
        P("row", "col", "layer", None, None),
        P("row", "col", "layer", None),
        P("row", "col", "layer", None, None, None),
        P("row", "col", "layer", None, None),
        P("row", "col", "layer", None, None),
        P("row", "col", "layer", None),
        P("row", "col", None, None),
    )
    out_specs = P("row", "col", "layer", None, None)
    return jax.shard_map(shards, mesh=mesh, in_specs=in_specs, out_specs=out_specs, check_vma=False)
```

```python
import functools

import jax
import jax.numpy as jnp
from jax import lax
from jax.experimental import pallas as pl
from jax.experimental.pallas import tpu as pltpu
from jax.sharding import PartitionSpec as P

BLOCK = 128
BATCH = 8
DEPTH = 4
SEMAPHORES = 128
PIECES = 3
MARKS_A = 12.1
MARKS_B = 12.1
LIST_AT = 157.0
B_PRIORITY = 0
MESH = pl.DeviceIdType.MESH


def own_marks(col, row, a_index, a_send, a_count, b_index, b_send, b_count):
    shape = (8, 128)
    place = lax.broadcasted_iota(jnp.int32, shape, 0) * 128 + lax.broadcasted_iota(
        jnp.int32, shape, 1
    )
    marks = jnp.zeros(shape, jnp.int32)
    for base, first, index, inner_at, send, count in (
        (0, col * a_index.shape[4], a_index, 1, a_send, a_count),
        (512, row * b_index.shape[4], b_index, 0, b_send, b_count),
    ):
        spread = 16 if inner_at else 8
        live = place < 0
        for d in range(send.shape[1]):
            for m in range(send.shape[0]):
                slot = jnp.where(m < count[0, 0, 0, d], base + first + send[m, d], -1)
                live = live | (place == slot)
        inner = jnp.zeros(shape, jnp.int32)
        for slot in range(index.shape[4]):
            k = index[0, 0, 0, inner_at, slot]
            other = index[0, 0, 0, 1 - inner_at, slot]
            inner = jnp.where(
                place == base + first + slot, lax.div(k, 32) * 8 + lax.rem(k, 8) + 1, inner
            )
            marks = jnp.where(place == base + 256 + first + slot, lax.div(other, spread), marks)
        marks = jnp.where(live, inner, marks)
    return marks


def product_list(a_marks, b_marks, c_index):
    kept = c_index.shape[3]
    a_sum = a_marks[0]
    for n in range(1, a_marks.shape[0]):
        a_sum = a_sum + a_marks[n]
    b_sum = b_marks[0]
    for n in range(1, b_marks.shape[0]):
        b_sum = b_sum + b_marks[n]
    square = (128, 128)
    sub = lax.broadcasted_iota(jnp.int32, square, 0)
    lane = lax.broadcasted_iota(jnp.int32, square, 1)
    sub_f, lane_f = sub.astype(jnp.float32), lane.astype(jnp.float32)
    eye = sub == lane

    def column(values):
        return jnp.sum(jnp.where(eye, values, 0.0), axis=1, keepdims=True)

    def line(values):
        return jnp.sum(jnp.where(eye, values, 0.0), axis=0, keepdims=True)

    a_f, b_f = a_sum.astype(jnp.float32), b_sum.astype(jnp.float32)
    c_code = [
        (lax.div(c_index[0, 0, 0, m], 16) * 64 + lax.div(c_index[0, 0, 1, m], 8)).astype(
            jnp.float32
        )
        for m in range(kept)
    ]
    entries = []
    for i in range(2):
        a_inner = column(a_f[i : i + 1])
        a_row = column(a_f[2 + i : 3 + i])
        first = jnp.full((128, 1), 65536.0, jnp.float32)
        last = jnp.full((128, 1), -1.0, jnp.float32)
        for j in range(2):
            b_inner, b_col = b_f[4 + j : 5 + j], b_f[6 + j : 7 + j]
            position = a_row * 64.0 + b_col
            slot = jnp.full(square, -1.0, jnp.float32)
            for m in range(kept):
                slot = jnp.where(position == c_code[m], float(m), slot)
            meets = (a_inner == b_inner) & (a_inner > 0.0) & (slot >= 0.0)
            key = (lane_f + 128.0 * j) * 32.0 + slot
            first = jnp.minimum(
                first, jnp.min(jnp.where(meets, key, 65536.0), axis=1, keepdims=True)
            )
            last = jnp.maximum(last, jnp.max(jnp.where(meets, key, -1.0), axis=1, keepdims=True))
        entries.append((i, last, last >= 0.0))
        entries.append((i, first, (last >= 0.0) & (first != last)))
    sub_1 = sub_f[:, :1]
    columns = []
    for n, (i, key, there) in enumerate(entries):
        slot = key - 32.0 * jnp.floor(key * (1.0 / 32.0))
        order = jnp.where(there, slot * 512.0 + (sub_1 + 128.0 * n), 65536.0)
        value = jnp.where(there, (sub_1 + 128.0 * i) * 8192.0 + key, 0.0)
        columns.append((there, order, value))
    lines = [line(order) for _, order, _ in columns]
    listed = [jnp.zeros((1, 128), jnp.float32) for _ in range(3)]
    count = jnp.zeros((1, 1), jnp.float32)
    for there, order, value in columns:
        rank = jnp.zeros((128, 1), jnp.float32)
        for other in lines:
            rank = rank + jnp.sum(jnp.where(other < order, 1.0, 0.0), axis=1, keepdims=True)
        rank = jnp.where(there, rank, -1.0)
        for n in range(3):
            listed[n] = listed[n] + jnp.sum(
                jnp.where(rank == lane_f + 128.0 * n, value, 0.0), axis=0, keepdims=True
            )
        count = count + jnp.sum(jnp.where(there, 1.0, 0.0), axis=0, keepdims=True)
    rows = jnp.concatenate(
        [jnp.where(lane_f[:1] + 128.0 * n < count, listed[n], float(kept)) for n in range(3)]
        + [jnp.broadcast_to(count, (1, 128)), jnp.zeros((4, 128), jnp.float32)],
        axis=0,
    ).astype(jnp.int32)
    return (
        lax.shift_right_logical(rows, 13),
        lax.shift_right_logical(rows, 5) & 255,
        rows & 31,
        rows,
    )


def product_kernel(
    list_ref, a_ref, b_ref, out_ref, a_buffer, b_buffer, total, a_sem, b_sem
):
    kept = out_ref.shape[0]
    batches = lax.div(list_ref[3, 3, 0] + (BATCH - 1), BATCH)

    def listed(part, batch):
        first = batch * BATCH
        row, lane = lax.shift_right_logical(first, 7), first & 127
        return [list_ref[part, row, lane + n] for n in range(BATCH)]

    def fetch(batch):
        spot = batch & (DEPTH - 1)
        a_spots, b_spots = listed(0, batch), listed(1, batch)
        for n in range(BATCH):
            pltpu.make_async_copy(
                a_ref.at[a_spots[n]], a_buffer.at[spot, n], a_sem.at[spot]
            ).start()
            pltpu.make_async_copy(
                b_ref.at[b_spots[n]], b_buffer.at[spot, n], b_sem.at[spot]
            ).start(B_PRIORITY)

    def prefetch(batch, carry):
        fetch(batch)
        return carry

    lax.fori_loop(0, jnp.minimum(batches, DEPTH), prefetch, 0)
    total[...] = jnp.zeros_like(total)

    def work(batch, carry):
        spot = batch & (DEPTH - 1)
        pltpu.make_async_copy(a_buffer.at[spot], a_buffer.at[spot], a_sem.at[spot]).wait()
        pltpu.make_async_copy(b_buffer.at[spot], b_buffer.at[spot], b_sem.at[spot]).wait()
        products = [
            jnp.dot(
                a_buffer[spot, n], b_buffer[spot, n], preferred_element_type=jnp.float32
            )
            for n in range(BATCH)
        ]
        slots = listed(2, batch)
        for n in range(BATCH):
            total[slots[n]] += products[n]

        @pl.when(batch + DEPTH < batches)
        def _():
            fetch(batch + DEPTH)

        return carry

    lax.fori_loop(0, batches, work, 0)
    out_ref[...] = total[0:kept].astype(out_ref.dtype)


def partial_product(listed, a_all, b_all, kept):
    smem = pl.BlockSpec(memory_space=pltpu.SMEM)
    anywhere = pl.BlockSpec(memory_space=pl.ANY)
    return pl.pallas_call(
        product_kernel,
        out_shape=jax.ShapeDtypeStruct((kept, BLOCK, BLOCK), jnp.bfloat16),
        in_specs=[smem, anywhere, anywhere],
        out_specs=pl.BlockSpec(memory_space=pltpu.VMEM),
        scratch_shapes=[
            pltpu.VMEM((DEPTH, BATCH, BLOCK, BLOCK), jnp.bfloat16),
            pltpu.VMEM((DEPTH, BATCH, BLOCK, BLOCK), jnp.bfloat16),
            pltpu.VMEM((kept + 1, BLOCK, BLOCK), jnp.float32),
            pltpu.SemaphoreType.DMA((DEPTH,)),
            pltpu.SemaphoreType.DMA((DEPTH,)),
        ],
        compiler_params=pltpu.CompilerParams(vmem_limit_bytes=60 << 20),
        name="partial_product",
    )(listed, a_all, b_all)


A_CHUNKS = ((0, 6, 1), (6, 6, 1), (12, 6, -1), (18, 6, -1))
B_CHUNKS = ((0, 5, 1, True), (5, 4, -1, True), (9, 3, 1, False), (12, 4, -1, False))


def gather_kernel(
    a_ref,
    b_ref,
    *rest,
):
    tables, (a_all, b_all, list_ref, m_ref, a_marks, b_marks) = rest[:7], rest[7:13]
    send_sem, recv_sem, own_sem = rest[13:16]
    scalars = rest[16:]
    loads = [
        pltpu.make_async_copy(table, held, own_sem.at[2 + n])
        for n, (table, held) in enumerate(zip(tables, scalars))
    ]
    for load in loads:
        load.start()
    a_index, a_send, a_count, b_index, b_send, b_count, c_index = scalars
    col, row = lax.axis_index("col"), lax.axis_index("row")
    a_ring, b_ring = lax.axis_size("col"), lax.axis_size("row") // 2
    plane, spot = row // b_ring, row % b_ring
    partner = row + b_ring - 2 * b_ring * plane

    def a_peer(way):
        return {"col": lax.rem(col + way + a_ring, a_ring)}

    def b_peer(way):
        return {"row": plane * b_ring + lax.rem(spot + way + b_ring, b_ring)}

    barrier = pltpu.get_barrier_semaphore()
    peers = (a_peer(1), a_peer(-1), b_peer(1), b_peer(-1), {"row": partner})
    for peer in peers:
        pl.semaphore_signal(barrier, inc=1, device_id=peer, device_id_type=MESH)
    pl.semaphore_wait(barrier, len(peers))

    numbers = {}
    sent = []

    def number(name):
        return numbers.setdefault(name, len(numbers))

    def send(name, source, target, peer):
        at = number(name)
        copy = pltpu.make_async_remote_copy(
            src_ref=source,
            dst_ref=target,
            send_sem=send_sem.at[at],
            recv_sem=recv_sem.at[at],
            device_id=peer,
            device_id_type=MESH,
        )
        copy.start()
        sent.append(copy)

    def arrive(name, target, peer):
        at = number(name)
        pltpu.make_async_remote_copy(
            src_ref=target,
            dst_ref=target,
            send_sem=send_sem.at[at],
            recv_sem=recv_sem.at[at],
            device_id=peer,
            device_id_type=MESH,
        ).wait_recv()

    a_pieces = [("marks", lambda o: a_marks.at[o], m_ref, 1, 0.0)]
    for n, (start, size, way) in enumerate(A_CHUNKS):
        a_pieces.append(
            (
                f"a{n}",
                lambda o, start=start, size=size: a_all.at[o, pl.ds(start, size)],
                a_ref.at[pl.ds(start, size)],
                way,
                size,
            )
        )
    b_pieces = [("marks", lambda o: b_marks.at[o], m_ref, 1, 0.0, False)]
    for n, (start, size, way, later) in enumerate(B_CHUNKS):
        b_pieces.append(
            (
                f"b{n}",
                lambda o, start=start, size=size: b_all.at[o, pl.ds(start, size)],
                b_ref.at[pl.ds(start, size)],
                way,
                size,
                later,
            )
        )

    events = []

    def forward_a(piece, way, step, origin, source):
        last = a_ring // 2
        if step < last or (step == last and piece[3] == way):
            send(("a", piece[0], way, step), source, piece[1](origin), a_peer(way))

    def forward_b(piece, way, step, side, origin, source):
        last = b_ring // 2
        if step < last or (step == last and piece[3] == way):
            send(("b", piece[0], way, step, side), source, piece[1](origin), b_peer(way))

    def b_origin(side, place):
        return (plane if side == "own" else 1 - plane) * b_ring + place

    for piece in b_pieces[1:]:
        if not piece[5]:
            send(("x", piece[0], 0, 0), piece[2], piece[1](row), {"row": partner})

    def leave(ranks):
        for rank in ranks:
            for way in (1, -1):
                if rank < len(A_CHUNKS):
                    piece = a_pieces[1:][rank if way == 1 else -1 - rank]
                    forward_a(piece, way, 1, col, piece[2])
                if rank < len(B_CHUNKS):
                    piece = b_pieces[1:][rank if way == 1 else -1 - rank]
                    forward_b(piece, way, 1, "own", row, piece[2])

    leave(range(1))
    for load in loads:
        load.wait()
    m_ref[...] = own_marks(
        col, row, a_index, a_send.at[0, 0, :, 0], a_count, b_index, b_send.at[0, 0, 0], b_count
    )
    send(("x", "marks", 0, 0), m_ref, b_marks.at[row], {"row": partner})
    for way in (1, -1):
        forward_a(a_pieces[0], way, 1, col, m_ref)
        forward_b(b_pieces[0], way, 1, "own", row, m_ref)
    leave(range(1, max(len(A_CHUNKS), len(B_CHUNKS))))
    for piece in b_pieces[1:]:
        if piece[5]:
            send(("x", piece[0], 0, 0), piece[2], piece[1](row), {"row": partner})
    own = [
        pltpu.make_async_copy(a_ref, a_all.at[col], own_sem.at[0]),
        pltpu.make_async_copy(b_ref, b_all.at[row], own_sem.at[1]),
    ]
    for copy in own:
        copy.start()
    a_marks[col] = m_ref[...]
    b_marks[row] = m_ref[...]

    a_step = sum(piece[4] for piece in a_pieces)
    b_step = sum(piece[4] * (1 if piece[5] else 2) for piece in b_pieces)

    def arrive_a(piece, way, step):
        origin = lax.rem(col - way * step + a_ring, a_ring)
        place = piece[1](origin)
        arrive(("a", piece[0], way, step), place, a_peer(way))
        forward_a(piece, way, step + 1, origin, place)

    def arrive_b(piece, way, step, side):
        origin = b_origin(side, lax.rem(spot - way * step + b_ring, b_ring))
        place = piece[1](origin)
        arrive(("b", piece[0], way, step, side), place, b_peer(way))
        forward_b(piece, way, step + 1, side, origin, place)
        if piece[5]:
            send(("x", piece[0], way, step), place, place, {"row": partner})

    def arrive_x(piece, way, step):
        origin = b_origin("far", lax.rem(spot - way * step + b_ring, b_ring))
        place = piece[1](origin)
        arrive(("x", piece[0], way, step), place, {"row": partner})
        if step == 0 and not piece[5]:
            for on in (1, -1):
                forward_b(piece, on, 1, "far", origin, place)

    def expect(time, event, *about):
        events.append((time, functools.partial(event, *about)))

    for way in (1, -1):
        for step in range(1, a_ring // 2 + 1):
            done = (step - 1) * a_step
            if step < a_ring // 2 or a_pieces[0][3] == way:
                expect(2 * done + MARKS_A, arrive_a, a_pieces[0], way, step)
            for piece in a_pieces[1:][::way]:
                if step < a_ring // 2 or piece[3] == way:
                    done += piece[4]
                    expect(2 * done, arrive_a, piece, way, step)
        for step in range(1, b_ring // 2 + 1):
            done = (step - 1) * b_step
            if step < b_ring // 2 or b_pieces[0][3] == way:
                expect(2 * done + MARKS_B + 0.2, arrive_b, b_pieces[0], way, step, "own")
                expect(2 * done + MARKS_B + 0.4, arrive_b, b_pieces[0], way, step, "far")
            for side in ("own", "far"):
                for piece in b_pieces[1:][::way]:
                    if side == "far" and piece[5]:
                        continue
                    if step < b_ring // 2 or piece[3] == way:
                        done += piece[4]
                        expect(2 * done, arrive_b, piece, way, step, side)
                        if piece[5]:
                            expect(2 * done + 40, arrive_x, piece, way, step)
    x_done = 0
    expect(MARKS_B, arrive_x, b_pieces[0], 0, 0)
    for piece in b_pieces[1:]:
        if not piece[5]:
            x_done += piece[4]
            expect(3 * x_done, arrive_x, piece, 0, 0)
        else:
            expect(60, arrive_x, piece, 0, 0)

    def write_list():
        for n, part in enumerate(product_list(a_marks, b_marks, c_index)):
            list_ref[n] = part

    expect(LIST_AT, write_list)
    for _, event in sorted(events, key=lambda e: e[0]):
        event()
    for copy in own:
        copy.wait()
    for copy in sent:
        copy.wait_send()
    assert len(numbers) <= SEMAPHORES


def gathered(a_own, b_own, a_index, a_send, a_count, b_index, b_send, b_count, c_index):
    anywhere = pl.BlockSpec(memory_space=pl.ANY)
    tables = (a_index, a_send, a_count, b_index, b_send, b_count, c_index)
    cols, rows = lax.axis_size("col"), lax.axis_size("row")
    return pl.pallas_call(
        gather_kernel,
        out_shape=(
            jax.ShapeDtypeStruct((cols,) + a_own.shape, a_own.dtype),
            jax.ShapeDtypeStruct((rows,) + b_own.shape, b_own.dtype),
            jax.ShapeDtypeStruct((4, 8, 128), jnp.int32),
        ),
        in_specs=[anywhere] * (2 + len(tables)),
        out_specs=(anywhere, anywhere, pl.BlockSpec(memory_space=pltpu.VMEM)),
        scratch_shapes=[
            pltpu.VMEM((8, 128), jnp.int32),
            pltpu.VMEM((cols, 8, 128), jnp.int32),
            pltpu.VMEM((rows, 8, 128), jnp.int32),
            pltpu.SemaphoreType.DMA((SEMAPHORES,)),
            pltpu.SemaphoreType.DMA((SEMAPHORES,)),
            pltpu.SemaphoreType.DMA((2 + len(tables),)),
        ]
        + [pltpu.SMEM(table.shape, table.dtype) for table in tables],
        compiler_params=pltpu.CompilerParams(
            collective_id=0, has_side_effects=True, vmem_limit_bytes=60 << 20
        ),
        name="gather_blocks",
    )(a_own, b_own, *tables)


def layer_sum_kernel(
    partial_ref, near_ref, from_far, mine, from_sibling, pair, near, send_sem, recv_sem, own_sem
):
    layer = lax.axis_index("layer")
    share = near_ref.shape[0]
    piece = share // PIECES
    sibling = {"layer": layer + 1 - 2 * lax.rem(layer, 2)}
    far = {"layer": lax.rem(layer + 2, 4)}
    loads = [
        pltpu.make_async_copy(
            partial_ref.at[pl.ds(owner * share, share)], mine.at[n], own_sem.at[n]
        )
        for n, owner in enumerate((far["layer"], layer))
    ]
    for load in loads:
        load.start()
    barrier = pltpu.get_barrier_semaphore()
    for peer in (sibling, far):
        pl.semaphore_signal(barrier, inc=1, device_id=peer, device_id_type=MESH)
    pl.semaphore_wait(barrier, 2)

    def copy(n, source, target, peer):
        return pltpu.make_async_remote_copy(
            src_ref=source,
            dst_ref=target,
            send_sem=send_sem.at[n],
            recv_sem=recv_sem.at[n],
            device_id=peer,
            device_id_type=MESH,
        )

    on, across = [], []
    for n, owner in enumerate((lax.rem(sibling["layer"] + 2, 4), sibling["layer"])):
        for p in range(PIECES):
            on.append(
                copy(
                    n * PIECES + p,
                    partial_ref.at[pl.ds(owner * share + p * piece, piece)],
                    from_sibling.at[n, pl.ds(p * piece, piece)],
                    sibling,
                )
            )
            on[-1].start()
    loads[0].wait()
    for p in range(PIECES):
        at = pl.ds(p * piece, piece)
        on[p].wait_recv()
        pair[at] = (
            mine[0, at].astype(jnp.float32) + from_sibling[0, at].astype(jnp.float32)
        ).astype(pair.dtype)
        across.append(copy(2 * PIECES + p, pair.at[at], from_far.at[at], far))
        across[-1].start()
    loads[1].wait()
    for p in range(PIECES):
        at = pl.ds(p * piece, piece)
        on[PIECES + p].wait_recv()
        near[at] = mine[1, at].astype(jnp.float32) + from_sibling[1, at].astype(jnp.float32)
    store = pltpu.make_async_copy(near, near_ref, own_sem.at[2])
    store.start()
    for p in range(PIECES):
        across[p].wait_recv()
    store.wait()
    for sent in on + across:
        sent.wait_send()


def layer_sum(partial):
    share = (partial.shape[0] // lax.axis_size("layer"),) + partial.shape[1:]
    anywhere = pl.BlockSpec(memory_space=pl.ANY)
    near, far = pl.pallas_call(
        layer_sum_kernel,
        out_shape=(
            jax.ShapeDtypeStruct(share, jnp.float32),
            jax.ShapeDtypeStruct(share, partial.dtype),
        ),
        in_specs=[anywhere],
        out_specs=(anywhere, anywhere),
        scratch_shapes=[
            pltpu.VMEM((2,) + share, partial.dtype),
            pltpu.VMEM((2,) + share, partial.dtype),
            pltpu.VMEM(share, partial.dtype),
            pltpu.VMEM(share, jnp.float32),
            pltpu.SemaphoreType.DMA((3 * PIECES,)),
            pltpu.SemaphoreType.DMA((3 * PIECES,)),
            pltpu.SemaphoreType.DMA((3,)),
        ],
        compiler_params=pltpu.CompilerParams(
            collective_id=1, has_side_effects=True, vmem_limit_bytes=53 << 20
        ),
        name="layer_sum",
    )(partial)
    return (near + far.astype(jnp.float32)).astype(partial.dtype)


def shards(a_blocks, a_index, a_send, a_count, b_blocks, b_index, b_send, b_count, c_index):
    a_all, b_all, listed = gathered(
        a_blocks[0, 0, 0],
        b_blocks[0, 0, 0],
        a_index,
        jnp.transpose(a_send, (0, 1, 4, 2, 3)),
        a_count,
        b_index,
        jnp.transpose(b_send, (0, 1, 2, 4, 3)),
        b_count,
        c_index,
    )
    a_all = a_all.reshape(-1, BLOCK, BLOCK)
    b_all = b_all.reshape(-1, BLOCK, BLOCK)
    partial = partial_product(listed, a_all, b_all, c_index.shape[3])
    return layer_sum(partial)[None, None]


def solution(mesh):
    in_specs = (
        P("row", "col", "layer", None, None, None),
        P("row", "col", "layer", None, None),
        P("row", "col", "layer", None, None),
        P("row", "col", "layer", None),
        P("row", "col", "layer", None, None, None),
        P("row", "col", "layer", None, None),
        P("row", "col", "layer", None, None),
        P("row", "col", "layer", None),
        P("row", "col", None, None),
    )
    out_specs = P("row", "col", "layer", None, None)
    return jax.shard_map(shards, mesh=mesh, in_specs=in_specs, out_specs=out_specs, check_vma=False)
```

```python
import functools

import jax
import jax.numpy as jnp
from jax import lax
from jax.experimental import pallas as pl
from jax.experimental.pallas import tpu as pltpu
from jax.sharding import PartitionSpec as P

BLOCK = 128
BATCH = 8
DEPTH = 8
SEMAPHORES = 128
PIECES = 3
MARKS_A = 12.1
MARKS_B = 12.1
LIST_AT = 157.0
B_PRIORITY = 0
MESH = pl.DeviceIdType.MESH


def own_marks(col, row, a_index, a_send, a_count, b_index, b_send, b_count):
    shape = (8, 128)
    place = lax.broadcasted_iota(jnp.int32, shape, 0) * 128 + lax.broadcasted_iota(
        jnp.int32, shape, 1
    )
    marks = jnp.zeros(shape, jnp.int32)
    for base, first, index, inner_at, send, count in (
        (0, col * a_index.shape[4], a_index, 1, a_send, a_count),
        (512, row * b_index.shape[4], b_index, 0, b_send, b_count),
    ):
        spread = 16 if inner_at else 8
        live = place < 0
        for d in range(send.shape[1]):
            for m in range(send.shape[0]):
                slot = jnp.where(m < count[0, 0, 0, d], base + first + send[m, d], -1)
                live = live | (place == slot)
        inner = jnp.zeros(shape, jnp.int32)
        for slot in range(index.shape[4]):
            k = index[0, 0, 0, inner_at, slot]
            other = index[0, 0, 0, 1 - inner_at, slot]
            inner = jnp.where(
                place == base + first + slot, lax.div(k, 32) * 8 + lax.rem(k, 8) + 1, inner
            )
            marks = jnp.where(place == base + 256 + first + slot, lax.div(other, spread), marks)
        marks = jnp.where(live, inner, marks)
    return marks


def product_list(a_marks, b_marks, c_index):
    kept = c_index.shape[3]
    a_sum = a_marks[0]
    for n in range(1, a_marks.shape[0]):
        a_sum = a_sum + a_marks[n]
    b_sum = b_marks[0]
    for n in range(1, b_marks.shape[0]):
        b_sum = b_sum + b_marks[n]
    square = (128, 128)
    sub = lax.broadcasted_iota(jnp.int32, square, 0)
    lane = lax.broadcasted_iota(jnp.int32, square, 1)
    sub_f, lane_f = sub.astype(jnp.float32), lane.astype(jnp.float32)
    eye = sub == lane

    def column(values):
        return jnp.sum(jnp.where(eye, values, 0.0), axis=1, keepdims=True)

    def line(values):
        return jnp.sum(jnp.where(eye, values, 0.0), axis=0, keepdims=True)

    a_f, b_f = a_sum.astype(jnp.float32), b_sum.astype(jnp.float32)
    c_code = [
        (lax.div(c_index[0, 0, 0, m], 16) * 64 + lax.div(c_index[0, 0, 1, m], 8)).astype(
            jnp.float32
        )
        for m in range(kept)
    ]
    entries = []
    for i in range(2):
        a_inner = column(a_f[i : i + 1])
        a_row = column(a_f[2 + i : 3 + i])
        first = jnp.full((128, 1), 65536.0, jnp.float32)
        last = jnp.full((128, 1), -1.0, jnp.float32)
        for j in range(2):
            b_inner, b_col = b_f[4 + j : 5 + j], b_f[6 + j : 7 + j]
            position = a_row * 64.0 + b_col
            slot = jnp.full(square, -1.0, jnp.float32)
            for m in range(kept):
                slot = jnp.where(position == c_code[m], float(m), slot)
            meets = (a_inner == b_inner) & (a_inner > 0.0) & (slot >= 0.0)
            key = (lane_f + 128.0 * j) * 32.0 + slot
            first = jnp.minimum(
                first, jnp.min(jnp.where(meets, key, 65536.0), axis=1, keepdims=True)
            )
            last = jnp.maximum(last, jnp.max(jnp.where(meets, key, -1.0), axis=1, keepdims=True))
        entries.append((i, last, last >= 0.0))
        entries.append((i, first, (last >= 0.0) & (first != last)))
    sub_1 = sub_f[:, :1]
    columns = []
    for n, (i, key, there) in enumerate(entries):
        slot = key - 32.0 * jnp.floor(key * (1.0 / 32.0))
        order = jnp.where(there, slot * 512.0 + (sub_1 + 128.0 * n), 65536.0)
        value = jnp.where(there, (sub_1 + 128.0 * i) * 8192.0 + key, 0.0)
        columns.append((there, order, value))
    lines = [line(order) for _, order, _ in columns]
    listed = [jnp.zeros((1, 128), jnp.float32) for _ in range(3)]
    count = jnp.zeros((1, 1), jnp.float32)
    for there, order, value in columns:
        rank = jnp.zeros((128, 1), jnp.float32)
        for other in lines:
            rank = rank + jnp.sum(jnp.where(other < order, 1.0, 0.0), axis=1, keepdims=True)
        rank = jnp.where(there, rank, -1.0)
        for n in range(3):
            listed[n] = listed[n] + jnp.sum(
                jnp.where(rank == lane_f + 128.0 * n, value, 0.0), axis=0, keepdims=True
            )
        count = count + jnp.sum(jnp.where(there, 1.0, 0.0), axis=0, keepdims=True)
    rows = jnp.concatenate(
        [jnp.where(lane_f[:1] + 128.0 * n < count, listed[n], float(kept)) for n in range(3)]
        + [jnp.broadcast_to(count, (1, 128)), jnp.zeros((4, 128), jnp.float32)],
        axis=0,
    ).astype(jnp.int32)
    return (
        lax.shift_right_logical(rows, 13),
        lax.shift_right_logical(rows, 5) & 255,
        rows & 31,
        rows,
    )


def product_kernel(
    list_ref, a_ref, b_ref, out_ref, a_buffer, b_buffer, total, a_sem, b_sem
):
    kept = out_ref.shape[0]
    batches = lax.div(list_ref[3, 3, 0] + (BATCH - 1), BATCH)

    def listed(part, batch):
        first = batch * BATCH
        row, lane = lax.shift_right_logical(first, 7), first & 127
        return [list_ref[part, row, lane + n] for n in range(BATCH)]

    def fetch(batch):
        spot = batch & (DEPTH - 1)
        a_spots, b_spots = listed(0, batch), listed(1, batch)
        for n in range(BATCH):
            pltpu.make_async_copy(
                a_ref.at[a_spots[n]], a_buffer.at[spot, n], a_sem.at[spot]
            ).start()
            pltpu.make_async_copy(
                b_ref.at[b_spots[n]], b_buffer.at[spot, n], b_sem.at[spot]
            ).start(B_PRIORITY)

    def prefetch(batch, carry):
        fetch(batch)
        return carry

    lax.fori_loop(0, jnp.minimum(batches, DEPTH), prefetch, 0)
    total[...] = jnp.zeros_like(total)

    def work(batch, carry):
        spot = batch & (DEPTH - 1)
        pltpu.make_async_copy(a_buffer.at[spot], a_buffer.at[spot], a_sem.at[spot]).wait()
        pltpu.make_async_copy(b_buffer.at[spot], b_buffer.at[spot], b_sem.at[spot]).wait()
        products = [
            jnp.dot(
                a_buffer[spot, n], b_buffer[spot, n], preferred_element_type=jnp.float32
            )
            for n in range(BATCH)
        ]
        slots = listed(2, batch)
        for n in range(BATCH):
            total[slots[n]] += products[n]

        @pl.when(batch + DEPTH < batches)
        def _():
            fetch(batch + DEPTH)

        return carry

    lax.fori_loop(0, batches, work, 0)
    out_ref[...] = total[0:kept].astype(out_ref.dtype)


def partial_product(listed, a_all, b_all, kept):
    smem = pl.BlockSpec(memory_space=pltpu.SMEM)
    anywhere = pl.BlockSpec(memory_space=pl.ANY)
    return pl.pallas_call(
        product_kernel,
        out_shape=jax.ShapeDtypeStruct((kept, BLOCK, BLOCK), jnp.bfloat16),
        in_specs=[smem, anywhere, anywhere],
        out_specs=pl.BlockSpec(memory_space=pltpu.VMEM),
        scratch_shapes=[
            pltpu.VMEM((DEPTH, BATCH, BLOCK, BLOCK), jnp.bfloat16),
            pltpu.VMEM((DEPTH, BATCH, BLOCK, BLOCK), jnp.bfloat16),
            pltpu.VMEM((kept + 1, BLOCK, BLOCK), jnp.float32),
            pltpu.SemaphoreType.DMA((DEPTH,)),
            pltpu.SemaphoreType.DMA((DEPTH,)),
        ],
        compiler_params=pltpu.CompilerParams(vmem_limit_bytes=60 << 20),
        name="partial_product",
    )(listed, a_all, b_all)


A_CHUNKS = ((0, 6, 1), (6, 6, 1), (12, 6, -1), (18, 6, -1))
B_CHUNKS = ((0, 5, 1, True), (5, 4, -1, True), (9, 3, 1, False), (12, 4, -1, False))


def gather_kernel(
    a_ref,
    b_ref,
    *rest,
):
    tables, (a_all, b_all, list_ref, m_ref, a_marks, b_marks) = rest[:7], rest[7:13]
    send_sem, recv_sem, own_sem = rest[13:16]
    scalars = rest[16:]
    loads = [
        pltpu.make_async_copy(table, held, own_sem.at[2 + n])
        for n, (table, held) in enumerate(zip(tables, scalars))
    ]
    for load in loads:
        load.start()
    a_index, a_send, a_count, b_index, b_send, b_count, c_index = scalars
    col, row = lax.axis_index("col"), lax.axis_index("row")
    a_ring, b_ring = lax.axis_size("col"), lax.axis_size("row") // 2
    plane, spot = row // b_ring, row % b_ring
    partner = row + b_ring - 2 * b_ring * plane

    def a_peer(way):
        return {"col": lax.rem(col + way + a_ring, a_ring)}

    def b_peer(way):
        return {"row": plane * b_ring + lax.rem(spot + way + b_ring, b_ring)}

    barrier = pltpu.get_barrier_semaphore()
    peers = (a_peer(1), a_peer(-1), b_peer(1), b_peer(-1), {"row": partner})
    for peer in peers:
        pl.semaphore_signal(barrier, inc=1, device_id=peer, device_id_type=MESH)
    pl.semaphore_wait(barrier, len(peers))

    numbers = {}
    sent = []

    def number(name):
        return numbers.setdefault(name, len(numbers))

    def send(name, source, target, peer):
        at = number(name)
        copy = pltpu.make_async_remote_copy(
            src_ref=source,
            dst_ref=target,
            send_sem=send_sem.at[at],
            recv_sem=recv_sem.at[at],
            device_id=peer,
            device_id_type=MESH,
        )
        copy.start()
        sent.append(copy)

    def arrive(name, target, peer):
        at = number(name)
        pltpu.make_async_remote_copy(
            src_ref=target,
            dst_ref=target,
            send_sem=send_sem.at[at],
            recv_sem=recv_sem.at[at],
            device_id=peer,
            device_id_type=MESH,
        ).wait_recv()

    a_pieces = [("marks", lambda o: a_marks.at[o], m_ref, 1, 0.0)]
    for n, (start, size, way) in enumerate(A_CHUNKS):
        a_pieces.append(
            (
                f"a{n}",
                lambda o, start=start, size=size: a_all.at[o, pl.ds(start, size)],
                a_ref.at[pl.ds(start, size)],
                way,
                size,
            )
        )
    b_pieces = [("marks", lambda o: b_marks.at[o], m_ref, 1, 0.0, False)]
    for n, (start, size, way, later) in enumerate(B_CHUNKS):
        b_pieces.append(
            (
                f"b{n}",
                lambda o, start=start, size=size: b_all.at[o, pl.ds(start, size)],
                b_ref.at[pl.ds(start, size)],
                way,
                size,
                later,
            )
        )

    events = []

    def forward_a(piece, way, step, origin, source):
        last = a_ring // 2
        if step < last or (step == last and piece[3] == way):
            send(("a", piece[0], way, step), source, piece[1](origin), a_peer(way))

    def forward_b(piece, way, step, side, origin, source):
        last = b_ring // 2
        if step < last or (step == last and piece[3] == way):
            send(("b", piece[0], way, step, side), source, piece[1](origin), b_peer(way))

    def b_origin(side, place):
        return (plane if side == "own" else 1 - plane) * b_ring + place

    for piece in b_pieces[1:]:
        if not piece[5]:
            send(("x", piece[0], 0, 0), piece[2], piece[1](row), {"row": partner})

    def leave(ranks):
        for rank in ranks:
            for way in (1, -1):
                if rank < len(A_CHUNKS):
                    piece = a_pieces[1:][rank if way == 1 else -1 - rank]
                    forward_a(piece, way, 1, col, piece[2])
                if rank < len(B_CHUNKS):
                    piece = b_pieces[1:][rank if way == 1 else -1 - rank]
                    forward_b(piece, way, 1, "own", row, piece[2])

    leave(range(1))
    for load in loads:
        load.wait()
    m_ref[...] = own_marks(
        col, row, a_index, a_send.at[0, 0, :, 0], a_count, b_index, b_send.at[0, 0, 0], b_count
    )
    send(("x", "marks", 0, 0), m_ref, b_marks.at[row], {"row": partner})
    for way in (1, -1):
        forward_a(a_pieces[0], way, 1, col, m_ref)
        forward_b(b_pieces[0], way, 1, "own", row, m_ref)
    leave(range(1, max(len(A_CHUNKS), len(B_CHUNKS))))
    for piece in b_pieces[1:]:
        if piece[5]:
            send(("x", piece[0], 0, 0), piece[2], piece[1](row), {"row": partner})
    own = [
        pltpu.make_async_copy(a_ref, a_all.at[col], own_sem.at[0]),
        pltpu.make_async_copy(b_ref, b_all.at[row], own_sem.at[1]),
    ]
    for copy in own:
        copy.start()
    a_marks[col] = m_ref[...]
    b_marks[row] = m_ref[...]

    a_step = sum(piece[4] for piece in a_pieces)
    b_step = sum(piece[4] * (1 if piece[5] else 2) for piece in b_pieces)

    def arrive_a(piece, way, step):
        origin = lax.rem(col - way * step + a_ring, a_ring)
        place = piece[1](origin)
        arrive(("a", piece[0], way, step), place, a_peer(way))
        forward_a(piece, way, step + 1, origin, place)

    def arrive_b(piece, way, step, side):
        origin = b_origin(side, lax.rem(spot - way * step + b_ring, b_ring))
        place = piece[1](origin)
        arrive(("b", piece[0], way, step, side), place, b_peer(way))
        forward_b(piece, way, step + 1, side, origin, place)
        if piece[5]:
            send(("x", piece[0], way, step), place, place, {"row": partner})

    def arrive_x(piece, way, step):
        origin = b_origin("far", lax.rem(spot - way * step + b_ring, b_ring))
        place = piece[1](origin)
        arrive(("x", piece[0], way, step), place, {"row": partner})
        if step == 0 and not piece[5]:
            for on in (1, -1):
                forward_b(piece, on, 1, "far", origin, place)

    def expect(time, event, *about):
        events.append((time, functools.partial(event, *about)))

    for way in (1, -1):
        for step in range(1, a_ring // 2 + 1):
            done = (step - 1) * a_step
            if step < a_ring // 2 or a_pieces[0][3] == way:
                expect(2 * done + MARKS_A, arrive_a, a_pieces[0], way, step)
            for piece in a_pieces[1:][::way]:
                if step < a_ring // 2 or piece[3] == way:
                    done += piece[4]
                    expect(2 * done, arrive_a, piece, way, step)
        for step in range(1, b_ring // 2 + 1):
            done = (step - 1) * b_step
            if step < b_ring // 2 or b_pieces[0][3] == way:
                expect(2 * done + MARKS_B + 0.2, arrive_b, b_pieces[0], way, step, "own")
                expect(2 * done + MARKS_B + 0.4, arrive_b, b_pieces[0], way, step, "far")
            for side in ("own", "far"):
                for piece in b_pieces[1:][::way]:
                    if side == "far" and piece[5]:
                        continue
                    if step < b_ring // 2 or piece[3] == way:
                        done += piece[4]
                        expect(2 * done, arrive_b, piece, way, step, side)
                        if piece[5]:
                            expect(2 * done + 40, arrive_x, piece, way, step)
    x_done = 0
    expect(MARKS_B, arrive_x, b_pieces[0], 0, 0)
    for piece in b_pieces[1:]:
        if not piece[5]:
            x_done += piece[4]
            expect(3 * x_done, arrive_x, piece, 0, 0)
        else:
            expect(60, arrive_x, piece, 0, 0)

    def write_list():
        for n, part in enumerate(product_list(a_marks, b_marks, c_index)):
            list_ref[n] = part

    expect(LIST_AT, write_list)
    for _, event in sorted(events, key=lambda e: e[0]):
        event()
    for copy in own:
        copy.wait()
    for copy in sent:
        copy.wait_send()
    assert len(numbers) <= SEMAPHORES


def gathered(a_own, b_own, a_index, a_send, a_count, b_index, b_send, b_count, c_index):
    anywhere = pl.BlockSpec(memory_space=pl.ANY)
    tables = (a_index, a_send, a_count, b_index, b_send, b_count, c_index)
    cols, rows = lax.axis_size("col"), lax.axis_size("row")
    return pl.pallas_call(
        gather_kernel,
        out_shape=(
            jax.ShapeDtypeStruct((cols,) + a_own.shape, a_own.dtype),
            jax.ShapeDtypeStruct((rows,) + b_own.shape, b_own.dtype),
            jax.ShapeDtypeStruct((4, 8, 128), jnp.int32),
        ),
        in_specs=[anywhere] * (2 + len(tables)),
        out_specs=(anywhere, anywhere, pl.BlockSpec(memory_space=pltpu.VMEM)),
        scratch_shapes=[
            pltpu.VMEM((8, 128), jnp.int32),
            pltpu.VMEM((cols, 8, 128), jnp.int32),
            pltpu.VMEM((rows, 8, 128), jnp.int32),
            pltpu.SemaphoreType.DMA((SEMAPHORES,)),
            pltpu.SemaphoreType.DMA((SEMAPHORES,)),
            pltpu.SemaphoreType.DMA((2 + len(tables),)),
        ]
        + [pltpu.SMEM(table.shape, table.dtype) for table in tables],
        compiler_params=pltpu.CompilerParams(
            collective_id=0, has_side_effects=True, vmem_limit_bytes=60 << 20
        ),
        name="gather_blocks",
    )(a_own, b_own, *tables)


def layer_sum_kernel(
    partial_ref, near_ref, from_far, mine, from_sibling, pair, near, send_sem, recv_sem, own_sem
):
    layer = lax.axis_index("layer")
    share = near_ref.shape[0]
    piece = share // PIECES
    sibling = {"layer": layer + 1 - 2 * lax.rem(layer, 2)}
    far = {"layer": lax.rem(layer + 2, 4)}
    loads = [
        pltpu.make_async_copy(
            partial_ref.at[pl.ds(owner * share, share)], mine.at[n], own_sem.at[n]
        )
        for n, owner in enumerate((far["layer"], layer))
    ]
    for load in loads:
        load.start()
    barrier = pltpu.get_barrier_semaphore()
    for peer in (sibling, far):
        pl.semaphore_signal(barrier, inc=1, device_id=peer, device_id_type=MESH)
    pl.semaphore_wait(barrier, 2)

    def copy(n, source, target, peer):
        return pltpu.make_async_remote_copy(
            src_ref=source,
            dst_ref=target,
            send_sem=send_sem.at[n],
            recv_sem=recv_sem.at[n],
            device_id=peer,
            device_id_type=MESH,
        )

    on, across = [], []
    for n, owner in enumerate((lax.rem(sibling["layer"] + 2, 4), sibling["layer"])):
        for p in range(PIECES):
            on.append(
                copy(
                    n * PIECES + p,
                    partial_ref.at[pl.ds(owner * share + p * piece, piece)],
                    from_sibling.at[n, pl.ds(p * piece, piece)],
                    sibling,
                )
            )
            on[-1].start()
    loads[0].wait()
    for p in range(PIECES):
        at = pl.ds(p * piece, piece)
        on[p].wait_recv()
        pair[at] = (
            mine[0, at].astype(jnp.float32) + from_sibling[0, at].astype(jnp.float32)
        ).astype(pair.dtype)
        across.append(copy(2 * PIECES + p, pair.at[at], from_far.at[at], far))
        across[-1].start()
    loads[1].wait()
    for p in range(PIECES):
        at = pl.ds(p * piece, piece)
        on[PIECES + p].wait_recv()
        near[at] = mine[1, at].astype(jnp.float32) + from_sibling[1, at].astype(jnp.float32)
    store = pltpu.make_async_copy(near, near_ref, own_sem.at[2])
    store.start()
    for p in range(PIECES):
        across[p].wait_recv()
    store.wait()
    for sent in on + across:
        sent.wait_send()


def layer_sum(partial):
    share = (partial.shape[0] // lax.axis_size("layer"),) + partial.shape[1:]
    anywhere = pl.BlockSpec(memory_space=pl.ANY)
    near, far = pl.pallas_call(
        layer_sum_kernel,
        out_shape=(
            jax.ShapeDtypeStruct(share, jnp.float32),
            jax.ShapeDtypeStruct(share, partial.dtype),
        ),
        in_specs=[anywhere],
        out_specs=(anywhere, anywhere),
        scratch_shapes=[
            pltpu.VMEM((2,) + share, partial.dtype),
            pltpu.VMEM((2,) + share, partial.dtype),
            pltpu.VMEM(share, partial.dtype),
            pltpu.VMEM(share, jnp.float32),
            pltpu.SemaphoreType.DMA((3 * PIECES,)),
            pltpu.SemaphoreType.DMA((3 * PIECES,)),
            pltpu.SemaphoreType.DMA((3,)),
        ],
        compiler_params=pltpu.CompilerParams(
            collective_id=1, has_side_effects=True, vmem_limit_bytes=53 << 20
        ),
        name="layer_sum",
    )(partial)
    return (near + far.astype(jnp.float32)).astype(partial.dtype)


def shards(a_blocks, a_index, a_send, a_count, b_blocks, b_index, b_send, b_count, c_index):
    a_all, b_all, listed = gathered(
        a_blocks[0, 0, 0],
        b_blocks[0, 0, 0],
        a_index,
        jnp.transpose(a_send, (0, 1, 4, 2, 3)),
        a_count,
        b_index,
        jnp.transpose(b_send, (0, 1, 2, 4, 3)),
        b_count,
        c_index,
    )
    a_all = a_all.reshape(-1, BLOCK, BLOCK)
    b_all = b_all.reshape(-1, BLOCK, BLOCK)
    partial = partial_product(listed, a_all, b_all, c_index.shape[3])
    return layer_sum(partial)[None, None]


def solution(mesh):
    in_specs = (
        P("row", "col", "layer", None, None, None),
        P("row", "col", "layer", None, None),
        P("row", "col", "layer", None, None),
        P("row", "col", "layer", None),
        P("row", "col", "layer", None, None, None),
        P("row", "col", "layer", None, None),
        P("row", "col", "layer", None, None),
        P("row", "col", "layer", None),
        P("row", "col", None, None),
    )
    out_specs = P("row", "col", "layer", None, None)
    return jax.shard_map(shards, mesh=mesh, in_specs=in_specs, out_specs=out_specs, check_vma=False)
```
